32 devices in a mesh: doc: 4 (over y, x), ctx: 2 (over core), head: 4 (over z).
Axes of the slice: x: 2, y: 2, z: 4, core: 2. Of those that a mesh axis runs over, the one named last changes fastest.
Arguments:
- queries: bfloat16 [128, 16384], P(('doc', 'ctx'), 'head'), as said below
- doc_of: int32 [128, 1], P(('doc', 'ctx')), may hold values from 0 to 3; in each aligned block of 16 rows (0 to 15, 16 to 31, ...) at most 6 rows name the same one
- doc_lengths: int32 [4], replicated, may hold values from 512 to 2048, as said below
- rotated_key_levels: bfloat16 [4, 2048, 1024], P('doc', 'ctx', 'head'), may hold values from -8 to 7
- rotated_value_levels: bfloat16 [4, 2048, 1024], P('doc', 'ctx', 'head'), may hold values from -8 to 7
- key_level_scale: bfloat16 [4, 8, 2048], P('doc', 'head', 'ctx'), may hold values from 0.19921875 to 0.796875
- value_level_scale: bfloat16 [4, 8, 2048], P('doc', 'head', 'ctx'), may hold values from 0.099609375 to 0.3984375
Outputs:
- attended: bfloat16 [128, 16384], P(('doc', 'ctx'))
The draws below stay inside these ranges and needn't reach their ends.
Inputs may be any that keep to these rules, and one draw needn't show every extreme that they name: `queries`: query rows. `doc_of`: in the rows of one device no document is named by more than 6 requests, a bound that some block reaches. `doc_lengths`: some document is valid over all its positions.
All inputs are finite; a program needn't handle non-finite values.
Results may differ from the reference program's by a relative error of at most 0.02.
Values may be sent and summed in bfloat16 or wider, within the bound.
No kernel may reach another device: no remote copies, remote signals or barrier semaphores. Data moves between devices by JAX's collectives and lax.ppermute only.
A program may use at most 128 MiB of HBM per device.

```python
import math
import jax
import jax.numpy as jnp
import numpy as np
from jax import lax

QUERY_HEADS = 128
KEY_VALUE_HEADS = 8
HEAD_WIDTH = 128
REQ_DEV = 16
CAP = 6
DOCUMENT_COUNT = 4
TOKEN_POSITIONS = 2048
REQ = 128


def draw_queries(key, part):
    base = jnp.clip(jax.random.normal(key, (REQ, QUERY_HEADS * HEAD_WIDTH), jnp.float32), -6.0, 6.0)
    return base.astype(jnp.bfloat16)


def draw_doc_lengths(key, part):
    first = jax.random.fold_in(key, 11)
    second = jax.random.fold_in(key, 12)
    drawn = jax.random.randint(first, (DOCUMENT_COUNT,), TOKEN_POSITIONS // 4, TOKEN_POSITIONS + 1, jnp.int32)
    full_doc = jax.random.randint(second, (), 0, DOCUMENT_COUNT, jnp.int32)
    return jnp.where(jnp.arange(DOCUMENT_COUNT, dtype=jnp.int32) == full_doc, jnp.int32(TOKEN_POSITIONS), drawn).astype(jnp.int32)


def draw_rotated_key_levels(key, part):
    integer_levels = jax.random.randint(jax.random.fold_in(key, 21), (DOCUMENT_COUNT, TOKEN_POSITIONS, KEY_VALUE_HEADS * HEAD_WIDTH), -8, 8, jnp.int32)
    return integer_levels.astype(jnp.float32).astype(jnp.bfloat16)


def draw_rotated_value_levels(key, part):
    integer_levels = jax.random.randint(jax.random.fold_in(key, 22), (DOCUMENT_COUNT, TOKEN_POSITIONS, KEY_VALUE_HEADS * HEAD_WIDTH), -8, 8, jnp.int32)
    return integer_levels.astype(jnp.float32).astype(jnp.bfloat16)


def block_scale(key, dims, shards, smallest, largest):
    def one(axis_at, shards_of):
        draws = jax.random.uniform(jax.random.fold_in(jax.random.fold_in(key, 6), axis_at), (shards_of,), jnp.float32, smallest / len(shards), largest / len(shards))
        return jnp.repeat(jnp.exp(draws), dims[axis_at] // shards_of).reshape((-1,) + (1,) * (len(dims) - axis_at - 1))

    loudness = one(*shards[0])
    for cut in shards[1:]:
        loudness = loudness * one(*cut)
    return loudness


def shared_out(own_key, own, number, rows, amount, top, reach, skew):
    sequence = jax.random.permutation(own_key, amount)
    heavy_load, usual = load_shares(amount, rows * top, reach, skew, True), load_shares(amount, rows * top, reach, skew, False)
    places = jnp.arange(amount)

    def named(sizes, offset_by):
        used = int((sizes > 0).sum())
        fixed = max(1, used // 4)
        passed = fixed + (places - fixed + offset_by * (used - fixed)) % max(1, amount - fixed)
        return jnp.zeros((amount,), jnp.int32).at[sequence[jnp.where(places < fixed, places, passed)]].set(jnp.asarray(sizes, jnp.int32))

    sizes = jnp.where(number % 4 == 0, named(heavy_load, number // 4), named(usual, number - number // 4 - 1))
    mixed = jax.random.permutation(jax.random.fold_in(own, 3), amount)
    donor, taker = mixed[0:amount // 2 * 2:2], mixed[1:amount // 2 * 2:2]
    slack = jnp.minimum(sizes[donor] - 1, reach - sizes[taker]) // 2
    slack = jnp.where((donor == sequence[0]) | (taker == sequence[0]) | (sizes[taker] == 0), 0, jnp.maximum(slack, 0))
    passed = jax.random.randint(jax.random.fold_in(own, 4), (amount // 2,), 0, 1 << 20) % (slack + 1)
    sizes = sizes.at[donor].add(-passed).at[taker].add(passed)
    labels = jnp.searchsorted(jnp.cumsum(sizes), jnp.arange(rows * top), side="right").astype(jnp.int32)
    grid = labels.reshape(top, rows).T
    grid = grid[jax.random.permutation(jax.random.fold_in(own, 1), rows)]
    offset_by = jax.random.randint(jax.random.fold_in(own, 2), (rows, 1), 0, top)
    return jnp.take_along_axis(grid, (jnp.arange(top)[None, :] + offset_by) % top, axis=1)


def load_shares(count, total, reach, skew, full):
    weights = [(1 << 20) // math.isqrt(grade ** skew) + 1 for grade in range(1, count + 1)]
    largest = reach if full else min(reach, max(-(-total // count), total * weights[0] // sum(weights)))
    least = 1 if total - largest >= count - 1 else 0
    holding, surplus = [largest] + [least] * (count - 1), total - largest - least * (count - 1)
    while surplus > 0:
        candidates = [i for i in range(1, count) if holding[i] < largest] or [i for i in range(1, count) if holding[i] < reach]
        whole, left = sum([weights[i] for i in candidates]), surplus
        for i in candidates:
            extra = min(reach - holding[i], max(1, left * weights[i] // whole), surplus)
            holding[i] = holding[i] + extra
            surplus = surplus - extra
    return np.array(holding)


def setup_inputs(seed: int = 0) -> dict:
    key_list = jax.random.split(jax.random.key(seed), 8)
    queries = draw_queries(jax.random.fold_in(key_list[7], 71), 0)
    doc_of_keys = jax.random.split(jax.random.fold_in(key_list[1], 1), REQ // REQ_DEV)
    doc_of_turns = jax.random.permutation(jax.random.fold_in(key_list[1], 3), REQ // REQ_DEV)
    doc_of = jax.vmap(lambda own, number: shared_out(jax.random.fold_in(key_list[1], 2), own, number, REQ_DEV, DOCUMENT_COUNT, 1, CAP, 2))(doc_of_keys, doc_of_turns).reshape((REQ, 1))
    doc_lengths = draw_doc_lengths(jax.random.fold_in(key_list[7], 71), 0)
    rotated_key_levels = draw_rotated_key_levels(jax.random.fold_in(key_list[7], 71), 0)
    rotated_value_levels = draw_rotated_value_levels(jax.random.fold_in(key_list[7], 71), 0)
    key_level_scale = jnp.clip(jnp.exp(math.log(0.796875) - 1.3862944 * jax.random.uniform(key_list[5], (DOCUMENT_COUNT, KEY_VALUE_HEADS, TOKEN_POSITIONS), jnp.float32) ** block_scale(key_list[5], (DOCUMENT_COUNT, KEY_VALUE_HEADS, TOKEN_POSITIONS), ((0, 4), (1, 4), (2, 2)), -0.2, 0.2)), 0.19921875, 0.796875).astype(jnp.bfloat16)
    value_level_scale = jnp.clip(jnp.exp(math.log(0.3984375) - 1.3862944 * jax.random.uniform(key_list[6], (DOCUMENT_COUNT, KEY_VALUE_HEADS, TOKEN_POSITIONS), jnp.float32) ** block_scale(key_list[6], (DOCUMENT_COUNT, KEY_VALUE_HEADS, TOKEN_POSITIONS), ((0, 4), (1, 4), (2, 2)), -0.2, 0.2)), 0.099609375, 0.3984375).astype(jnp.bfloat16)
    return {"queries": queries, "doc_of": doc_of, "doc_lengths": doc_lengths, "rotated_key_levels": rotated_key_levels, "rotated_value_levels": rotated_value_levels, "key_level_scale": key_level_scale, "value_level_scale": value_level_scale}


def hadamard_signs():
    idx = jnp.arange(HEAD_WIDTH, dtype=jnp.int32)
    both = jnp.bitwise_and(idx[:, None], idx[None, :])
    parity = jnp.zeros_like(both)
    for bit in range(HEAD_WIDTH.bit_length()):
        parity = parity + jnp.bitwise_and(jnp.right_shift(both, bit), 1)
    return (1 - 2 * (parity % 2)).astype(jnp.float32)

def reference(queries, doc_of, doc_lengths, rotated_key_levels, rotated_value_levels, key_level_scale, value_level_scale):
    inverse_total = 1.0 / math.sqrt(HEAD_WIDTH)
    signs = hadamard_signs()
    head_group = QUERY_HEADS // KEY_VALUE_HEADS
    positions = jnp.arange(TOKEN_POSITIONS, dtype=jnp.int32)

    def single(item):
        query_row, document_index = item
        rotated_rows = (jnp.dot(query_row.reshape(QUERY_HEADS, HEAD_WIDTH), signs.astype(jnp.bfloat16), preferred_element_type=jnp.float32) * inverse_total).astype(jnp.bfloat16)
        rotated_rows = rotated_rows.astype(jnp.float32).reshape(KEY_VALUE_HEADS, head_group, HEAD_WIDTH)
        key_block = lax.dynamic_index_in_dim(rotated_key_levels, document_index, 0, keepdims=False).astype(jnp.float32).reshape(TOKEN_POSITIONS, KEY_VALUE_HEADS, HEAD_WIDTH)
        value_block = lax.dynamic_index_in_dim(rotated_value_levels, document_index, 0, keepdims=False).astype(jnp.float32).reshape(TOKEN_POSITIONS, KEY_VALUE_HEADS, HEAD_WIDTH)
        key_block_scale = lax.dynamic_index_in_dim(key_level_scale, document_index, 0, keepdims=False).astype(jnp.float32)
        value_block_scale = lax.dynamic_index_in_dim(value_level_scale, document_index, 0, keepdims=False).astype(jnp.float32)
        length = lax.dynamic_index_in_dim(doc_lengths, document_index, 0, keepdims=False)
        valid_mask = positions < length
        score_block = jnp.einsum('rpe,cre->rpc', rotated_rows, key_block, precision=lax.Precision.HIGHEST) * (key_block_scale * inverse_total)[:, None, :]
        score_block = jnp.where(valid_mask[None, None, :], score_block, jnp.float32(-1e+30))
        top = lax.optimization_barrier(jnp.max(score_block, axis=-1))
        probs = jnp.where(valid_mask[None, None, :], jnp.exp(score_block - top[..., None]), jnp.float32(0.0))
        total = lax.optimization_barrier(jnp.sum(probs, axis=-1))
        weights = (probs * value_block_scale[:, None, :]).astype(jnp.bfloat16).astype(jnp.float32)
        summed = jnp.einsum('kgs,skd->kgd', weights, value_block, precision=lax.Precision.HIGHEST)
        mixed = summed / total[..., None]
        result = jnp.einsum('kgd,de->kge', mixed, signs, precision=lax.Precision.HIGHEST) * inverse_total
        return result.astype(jnp.bfloat16).reshape(QUERY_HEADS * HEAD_WIDTH)
    return lax.map(single, (queries, doc_of[:, 0].astype(jnp.int32)))
```

```python
import functools
import math

import jax
import jax.numpy as jnp
from jax import lax
from jax.experimental import pallas as pl
from jax.experimental.pallas import tpu as pltpu
from jax.sharding import PartitionSpec as P

HEAD_WIDTH = 128
LANES = 128
VMEM_BYTES = 40 * 1024 * 1024


def peer_of(index, step, count):
    if count & (count - 1) == 0:
        return index ^ step
    return (index + step) % count


def sent(value, axis, step):
    count = lax.axis_size(axis)
    return lax.ppermute(value, axis, [(i, peer_of(i, step, count)) for i in range(count)])


def returned(value, axis, step):
    count = lax.axis_size(axis)
    return lax.ppermute(value, axis, [(peer_of(i, step, count), i) for i in range(count)])


def sign_matrix():
    row = lax.broadcasted_iota(jnp.int32, (HEAD_WIDTH, HEAD_WIDTH), 0)
    column = lax.broadcasted_iota(jnp.int32, (HEAD_WIDTH, HEAD_WIDTH), 1)
    both = row & column
    both = both ^ (both >> 4)
    both = both ^ (both >> 2)
    both = both ^ (both >> 1)
    return (1 - 2 * (both & 1)).astype(jnp.float32).astype(jnp.bfloat16)


def placing_matrix(doc_column, n_doc, cap):
    rows = doc_column.shape[0]
    group = LANES // rows
    me = lax.axis_index("doc")
    request = lax.broadcasted_iota(jnp.int32, (rows, LANES), 0)
    lane = lax.broadcasted_iota(jnp.int32, (rows, LANES), 1)
    docs = jnp.broadcast_to(doc_column, (rows, LANES))
    lane_request = lane % rows
    lane_doc = jnp.sum(jnp.where(request == lane_request, docs, 0), axis=0, keepdims=True)
    rank = jnp.sum(
        jnp.where((docs == lane_doc) & (request < lane_request), 1, 0), axis=0, keepdims=True
    )
    if n_doc & (n_doc - 1) == 0:
        step = lane_doc ^ me
    else:
        step = (lane_doc - me + n_doc) % n_doc
    place = step * (group * cap) + (lane[:1] // rows) * cap + rank
    slots = n_doc * group * cap
    slot = lax.broadcasted_iota(jnp.int32, (slots, LANES), 0)
    return jnp.where(slot == place, 1.0, 0.0).astype(jnp.bfloat16)


def dispatch_kernel(n_doc, cap, doc_ref, query_ref, *out_refs):
    rows, width = query_ref.shape
    group = LANES // rows
    heads = width // HEAD_WIDTH
    block = group * cap
    placing = placing_matrix(doc_ref[...], n_doc, cap)
    signs = sign_matrix()
    scale = 1.0 / math.sqrt(HEAD_WIDTH)
    for g in range(heads // group):
        stacked = jnp.concatenate(
            [
                query_ref[:, (g * group + h) * HEAD_WIDTH : (g * group + h + 1) * HEAD_WIDTH]
                for h in range(group)
            ],
            axis=0,
        )
        placed = jnp.dot(placing, stacked, preferred_element_type=jnp.float32).astype(jnp.bfloat16)
        rotated = jnp.dot(placed, signs, preferred_element_type=jnp.float32) * scale
        rotated = rotated.astype(jnp.bfloat16)
        for k in range(n_doc):
            out_refs[k][g * block : (g + 1) * block, :] = rotated[k * block : (k + 1) * block]


def collect_kernel(n_doc, cap, doc_ref, *refs):
    back_refs, out_ref = refs[:n_doc], refs[n_doc]
    rows, width = out_ref.shape
    group = LANES // rows
    heads = width // HEAD_WIDTH
    block = group * cap
    placing = placing_matrix(doc_ref[...], n_doc, cap)
    for g in range(heads // group):
        slots = jnp.concatenate(
            [back_refs[k][g * block : (g + 1) * block, :] for k in range(n_doc)], axis=0
        )
        mine = lax.dot_general(
            placing, slots, (((0,), (0,)), ((), ())), preferred_element_type=jnp.float32
        ).astype(jnp.bfloat16)
        for h in range(group):
            at = (g * group + h) * HEAD_WIDTH
            out_ref[:, at : at + HEAD_WIDTH] = mine[h * rows : (h + 1) * rows]


def attend_kernel(n_doc, n_ctx, kv_dev, length_ref, *refs):
    query_refs, refs = refs[:n_doc], refs[n_doc:]
    cache_refs, out_refs = refs[: 4 * n_ctx], refs[4 * n_ctx :]
    my_ctx = lax.axis_index("ctx")
    length = length_ref[lax.axis_index("doc")]
    shard_len = cache_refs[0].shape[0]
    rows_doc = query_refs[0].shape[0] // kv_dev
    signs = sign_matrix()
    scale = 1.0 / math.sqrt(HEAD_WIDTH)
    position = lax.broadcasted_iota(jnp.int32, (1, shard_len), 1)
    for g in range(kv_dev):
        span = slice(g * rows_doc, (g + 1) * rows_doc)
        head = slice(g * HEAD_WIDTH, (g + 1) * HEAD_WIDTH)
        query_rows = jnp.concatenate([ref[span, :] for ref in query_refs], axis=0)
        state = None
        for first in range(0, n_ctx, 2):
            steps = range(first, min(first + 2, n_ctx))
            scores = []
            for step in steps:
                key_ref, key_scale_ref = cache_refs[4 * step], cache_refs[4 * step + 2]
                anchor = lax.rem(my_ctx - step + n_ctx, n_ctx) * shard_len
                key_scale = key_scale_ref[g : g + 1, :].astype(jnp.float32) * (
                    scale * math.log2(math.e)
                )
                shift = jnp.where(position + anchor < length, 0.0, -1e30)
                product = lax.dot_general(
                    query_rows,
                    key_ref[:, head],
                    (((1,), (1,)), ((), ())),
                    preferred_element_type=jnp.float32,
                )
                scores.append(product * key_scale + shift)
            top = functools.reduce(
                jnp.maximum, [jnp.max(score, axis=-1, keepdims=True) for score in scores]
            )
            if state is not None:
                top = jnp.maximum(top, state[0])
            total, summed = 0.0, 0.0
            for step, score in zip(steps, scores):
                value_ref, value_scale_ref = cache_refs[4 * step + 1], cache_refs[4 * step + 3]
                value_scale = value_scale_ref[g : g + 1, :].astype(jnp.float32)
                probs = jnp.exp2(score - top)
                total = total + jnp.sum(probs, axis=-1, keepdims=True)
                weights = (probs * value_scale).astype(jnp.bfloat16)
                summed = summed + jnp.dot(
                    weights, value_ref[:, head], preferred_element_type=jnp.float32
                )
            if state is not None:
                factor = jnp.exp2(state[0] - top)
                total = total + state[1] * factor
                summed = summed + state[2] * factor
            state = (top, total, summed)
        mixed = state[2] * (scale / state[1])
        high = mixed.astype(jnp.bfloat16)
        low = (mixed - high.astype(jnp.float32)).astype(jnp.bfloat16)
        result = jnp.dot(high, signs, preferred_element_type=jnp.float32) + jnp.dot(
            low, signs, preferred_element_type=jnp.float32
        )
        result = result.astype(jnp.bfloat16)
        for k in range(n_doc):
            out_refs[k][span, :] = result[k * rows_doc : (k + 1) * rows_doc]


def assemble_kernel(n_head, *refs):
    block_refs, out_ref, sems = refs[:n_head], refs[n_head], refs[n_head + 1]
    me = lax.axis_index("head")
    width = block_refs[0].shape[1]
    copies = []
    for step in range(n_head):
        at = pl.multiple_of(peer_of_traced(me, step, n_head) * width, width)
        copies.append(
            pltpu.make_async_copy(block_refs[step], out_ref.at[:, pl.ds(at, width)], sems.at[step])
        )
    for copy in copies:
        copy.start()
    for copy in copies:
        copy.wait()


def peer_of_traced(index, step, count):
    if count & (count - 1) == 0:
        return index ^ step
    return lax.rem(index + step, count)


def shards(
    queries,
    doc_of,
    doc_lengths,
    rotated_key_levels,
    rotated_value_levels,
    key_level_scale,
    value_level_scale,
):
    rows_home, width = queries.shape
    heads_dev = width // HEAD_WIDTH
    kv_dev = key_level_scale.shape[1]
    shard_len = rotated_key_levels.shape[1]
    n_doc = lax.axis_size("doc")
    n_ctx = lax.axis_size("ctx")
    n_head = lax.axis_size("head")
    cap = max(2, 3 * rows_home // (2 * n_doc))
    params = pltpu.CompilerParams(vmem_limit_bytes=VMEM_BYTES)
    vmem = pl.BlockSpec(memory_space=pltpu.VMEM)
    slots = heads_dev * cap
    slot_block = jax.ShapeDtypeStruct((slots, HEAD_WIDTH), jnp.bfloat16)

    own = (rotated_key_levels[0], rotated_value_levels[0], key_level_scale[0], value_level_scale[0])
    cache = list(own)
    for step in range(1, n_ctx):
        pairs = [(i, (i + step) % n_ctx) for i in range(n_ctx)]
        cache += [lax.ppermute(part, "ctx", pairs) for part in own]

    outgoing = pl.pallas_call(
        functools.partial(dispatch_kernel, n_doc, cap),
        out_shape=[slot_block] * n_doc,
        in_specs=[vmem, vmem],
        out_specs=[vmem] * n_doc,
        compiler_params=params,
    )(doc_of, queries)
    arrived = [outgoing[0]] + [sent(outgoing[k], "doc", k) for k in range(1, n_doc)]

    rows = n_doc * slots
    finished = pl.pallas_call(
        functools.partial(attend_kernel, n_doc, n_ctx, kv_dev),
        out_shape=[slot_block] * n_doc,
        in_specs=[pl.BlockSpec(memory_space=pltpu.SMEM)] + [vmem] * (n_doc + 4 * n_ctx),
        out_specs=[vmem] * n_doc,
        compiler_params=params,
        cost_estimate=pl.CostEstimate(
            flops=4 * rows * n_ctx * shard_len * HEAD_WIDTH,
            bytes_accessed=4 * n_ctx * shard_len * kv_dev * HEAD_WIDTH,
            transcendentals=rows * n_ctx * shard_len,
        ),
    )(doc_lengths, *arrived, *cache)
    back = [finished[0]] + [returned(finished[k], "doc", k) for k in range(1, n_doc)]

    mine = pl.pallas_call(
        functools.partial(collect_kernel, n_doc, cap),
        out_shape=jax.ShapeDtypeStruct((rows_home, width), jnp.bfloat16),
        in_specs=[vmem] * (1 + n_doc),
        out_specs=vmem,
        compiler_params=params,
    )(doc_of, *back)

    blocks = [mine] + [returned(mine, "head", step) for step in range(1, n_head)]
    hbm = pl.BlockSpec(memory_space=pl.ANY)
    return pl.pallas_call(
        functools.partial(assemble_kernel, n_head),
        out_shape=jax.ShapeDtypeStruct((rows_home, n_head * width), jnp.bfloat16),
        in_specs=[hbm] * n_head,
        out_specs=hbm,
        scratch_shapes=[pltpu.SemaphoreType.DMA((n_head,))],
        compiler_params=params,
    )(*blocks)


def solution(mesh):
    in_specs = (
        P(("doc", "ctx"), "head"),
        P(("doc", "ctx"), None),
        P(),
        P("doc", "ctx", "head"),
        P("doc", "ctx", "head"),
        P("doc", "head", "ctx"),
        P("doc", "head", "ctx"),
    )
    out_specs = P(("doc", "ctx"), None)
    return jax.shard_map(shards, mesh=mesh, in_specs=in_specs, out_specs=out_specs, check_vma=False)
```

```python
import functools
import math

import jax
import jax.numpy as jnp
from jax import lax
from jax.experimental import pallas as pl
from jax.experimental.pallas import tpu as pltpu
from jax.sharding import PartitionSpec as P

HEAD_WIDTH = 128
LANES = 128
VMEM_BYTES = 40 * 1024 * 1024


def peer_of(index, step, count):
    if count & (count - 1) == 0:
        return index ^ step
    return (index + step) % count


def sent(value, axis, step):
    count = lax.axis_size(axis)
    return lax.ppermute(value, axis, [(i, peer_of(i, step, count)) for i in range(count)])


def returned(value, axis, step):
    count = lax.axis_size(axis)
    return lax.ppermute(value, axis, [(peer_of(i, step, count), i) for i in range(count)])


def sign_matrix():
    row = lax.broadcasted_iota(jnp.int32, (HEAD_WIDTH, HEAD_WIDTH), 0)
    column = lax.broadcasted_iota(jnp.int32, (HEAD_WIDTH, HEAD_WIDTH), 1)
    both = row & column
    both = both ^ (both >> 4)
    both = both ^ (both >> 2)
    both = both ^ (both >> 1)
    return (1 - 2 * (both & 1)).astype(jnp.float32).astype(jnp.bfloat16)


def placing_matrix(doc_row, n_doc, cap):
    rows = doc_row.shape[1]
    group = LANES // rows
    me = lax.axis_index("doc")
    square = (rows, rows)
    diagonal = lax.broadcasted_iota(jnp.int32, square, 0) == lax.broadcasted_iota(
        jnp.int32, square, 1
    )
    doc_column = jnp.sum(
        jnp.where(diagonal, jnp.broadcast_to(doc_row, square), 0), axis=1, keepdims=True
    )
    request = lax.broadcasted_iota(jnp.int32, (rows, LANES), 0)
    lane = lax.broadcasted_iota(jnp.int32, (rows, LANES), 1)
    docs = jnp.broadcast_to(doc_column, (rows, LANES))
    lane_request = lane % rows
    lane_doc = jnp.sum(jnp.where(request == lane_request, docs, 0), axis=0, keepdims=True)
    rank = jnp.sum(
        jnp.where((docs == lane_doc) & (request < lane_request), 1, 0), axis=0, keepdims=True
    )
    if n_doc & (n_doc - 1) == 0:
        step = lane_doc ^ me
    else:
        step = (lane_doc - me + n_doc) % n_doc
    place = step * (group * cap) + (lane[:1] // rows) * cap + rank
    slots = n_doc * group * cap
    slot = lax.broadcasted_iota(jnp.int32, (slots, LANES), 0)
    return jnp.where(slot == place, 1.0, 0.0).astype(jnp.bfloat16)


def dispatch_kernel(
    n_doc,
    n_ctx,
    cap,
    doc_hbm,
    length_hbm,
    query_hbm,
    key_hbm,
    value_hbm,
    key_scale_hbm,
    value_scale_hbm,
    placing_ref,
    shift_ref,
    scales_ref,
    key_ref,
    value_ref,
    *refs,
):
    out_refs, (doc_ref, length_ref, query_ref, key_scale_ref, value_scale_ref, sems) = (
        refs[:n_doc],
        refs[n_doc:],
    )
    pairs = (
        (doc_hbm, doc_ref),
        (query_hbm, query_ref),
        (length_hbm, length_ref),
        (key_scale_hbm, key_scale_ref),
        (value_scale_hbm, value_scale_ref),
        (key_hbm, key_ref),
        (value_hbm, value_ref),
    )
    copies = [
        pltpu.make_async_copy(source, target, sems.at[at])
        for at, (source, target) in enumerate(pairs)
    ]
    for copy in copies:
        copy.start()
    rows, width = query_ref.shape
    group = LANES // rows
    heads = width // HEAD_WIDTH
    block = group * cap
    signs = sign_matrix()
    scale = 1.0 / math.sqrt(HEAD_WIDTH)
    copies[0].wait()
    placing = placing_matrix(doc_ref[...], n_doc, cap)
    placing_ref[...] = placing
    copies[1].wait()
    rotated = []
    for g in range(heads // group):
        stacked = jnp.concatenate(
            [
                query_ref[:, (g * group + h) * HEAD_WIDTH : (g * group + h + 1) * HEAD_WIDTH]
                for h in range(group)
            ],
            axis=0,
        )
        product = jnp.dot(stacked, signs, preferred_element_type=jnp.float32) * scale
        rotated.append(product.astype(jnp.bfloat16))
    for g in range(heads // group):
        placed = jnp.dot(placing, rotated[g], preferred_element_type=jnp.float32).astype(
            jnp.bfloat16
        )
        for k in range(n_doc):
            out_refs[k][g * block : (g + 1) * block, :] = placed[k * block : (k + 1) * block]
    for copy in copies[2:5]:
        copy.wait()
    scales_ref[...] = jnp.concatenate(
        [key_scale_ref[...].astype(jnp.float32), value_scale_ref[...].astype(jnp.float32)], axis=0
    ).astype(jnp.bfloat16)
    lengths = length_ref[...]
    lane = lax.broadcasted_iota(jnp.int32, lengths.shape, 1)
    length = jnp.sum(
        jnp.where(lane == lax.axis_index("doc"), lengths, 0), axis=1, keepdims=True
    )
    shard_len = key_ref.shape[0]
    step = lax.broadcasted_iota(jnp.int32, shift_ref.shape, 0)
    anchor = (lax.axis_index("ctx") - step + n_ctx) % n_ctx
    position = lax.broadcasted_iota(jnp.int32, shift_ref.shape, 1) + anchor * shard_len
    shift_ref[...] = jnp.where(position < length, 0.0, -1e30)
    for copy in copies[5:]:
        copy.wait()


def collect_kernel(n_doc, cap, placing_ref, *refs):
    back_refs, out_ref = refs[:n_doc], refs[n_doc]
    rows, width = out_ref.shape
    group = LANES // rows
    heads = width // HEAD_WIDTH
    block = group * cap
    placing = placing_ref[...]
    for g in range(heads // group):
        slots = jnp.concatenate(
            [back_refs[k][g * block : (g + 1) * block, :] for k in range(n_doc)], axis=0
        )
        mine = lax.dot_general(
            placing, slots, (((0,), (0,)), ((), ())), preferred_element_type=jnp.float32
        ).astype(jnp.bfloat16)
        for h in range(group):
            at = (g * group + h) * HEAD_WIDTH
            out_ref[:, at : at + HEAD_WIDTH] = mine[h * rows : (h + 1) * rows]


def attend_kernel(sources, n_ctx, kv_dev, shift_ref, *refs):
    query_refs, refs = refs[:sources], refs[sources:]
    cache_refs, out_refs = refs[: 3 * n_ctx], refs[3 * n_ctx :]
    rows_doc = query_refs[0].shape[0] // kv_dev
    signs = sign_matrix()
    scale = 1.0 / math.sqrt(HEAD_WIDTH)
    groups = range(kv_dev)
    spans = [slice(g * rows_doc, (g + 1) * rows_doc) for g in groups]
    heads = [slice(g * HEAD_WIDTH, (g + 1) * HEAD_WIDTH) for g in groups]
    rows = [jnp.concatenate([ref[span, :] for ref in query_refs], axis=0) for span in spans]
    states = [None] * kv_dev
    for first in range(0, n_ctx, 2):
        steps = range(first, min(first + 2, n_ctx))
        scores = {}
        for g in groups:
            for step in steps:
                key_ref, scales_ref = cache_refs[3 * step], cache_refs[3 * step + 2]
                key_scale = scales_ref[g : g + 1, :].astype(jnp.float32) * (
                    scale * math.log2(math.e)
                )
                product = lax.dot_general(
                    rows[g],
                    key_ref[:, heads[g]],
                    (((1,), (1,)), ((), ())),
                    preferred_element_type=jnp.float32,
                )
                scores[g, step] = product * key_scale + shift_ref[step : step + 1, :]
        tops = []
        for g in groups:
            top = functools.reduce(
                jnp.maximum, [jnp.max(scores[g, step], axis=-1, keepdims=True) for step in steps]
            )
            tops.append(top if states[g] is None else jnp.maximum(top, states[g][0]))
        for g in groups:
            all_probs, summed = 0.0, 0.0
            for step in steps:
                value_ref, scales_ref = cache_refs[3 * step + 1], cache_refs[3 * step + 2]
                value_scale = scales_ref[kv_dev + g : kv_dev + g + 1, :].astype(jnp.float32)
                probs = jnp.exp2(scores[g, step] - tops[g])
                all_probs = all_probs + probs
                weights = (probs * value_scale).astype(jnp.bfloat16)
                summed = summed + jnp.dot(
                    weights, value_ref[:, heads[g]], preferred_element_type=jnp.float32
                )
            total = jnp.sum(all_probs, axis=-1, keepdims=True)
            if states[g] is not None:
                factor = jnp.exp2(states[g][0] - tops[g])
                total = total + states[g][1] * factor
                summed = summed + states[g][2] * factor
            states[g] = (tops[g], total, summed)
    for g in groups:
        _, total, summed = states[g]
        mixed = summed * (scale / total)
        high = mixed.astype(jnp.bfloat16)
        low = (mixed - high.astype(jnp.float32)).astype(jnp.bfloat16)
        result = jnp.dot(high, signs, preferred_element_type=jnp.float32) + jnp.dot(
            low, signs, preferred_element_type=jnp.float32
        )
        result = result.astype(jnp.bfloat16)
        for k in range(sources):
            out_refs[k][spans[g], :] = result[k * rows_doc : (k + 1) * rows_doc]


def assemble_kernel(n_head, places, *refs):
    block_refs, out_ref, sems = refs[: len(places)], refs[-2], refs[-1]
    me, parity = lax.axis_index("head"), lax.rem(lax.axis_index("ctx"), 2)
    width = block_refs[0].shape[1]
    copies = []
    for at, (step, wanted) in enumerate(places):
        column = pl.multiple_of(peer_of_traced(me, step, n_head) * width, width)
        copy = pltpu.make_async_copy(
            block_refs[at], out_ref.at[:, pl.ds(column, width)], sems.at[at]
        )
        copies.append((copy, wanted))
    for copy, wanted in copies:
        if wanted is None:
            copy.start()
        else:
            pl.when(parity == wanted)(copy.start)
    for copy, wanted in copies:
        if wanted is None:
            copy.wait()
        else:
            pl.when(parity == wanted)(copy.wait)


def peer_of_traced(index, step, count):
    if count & (count - 1) == 0:
        return index ^ step
    return lax.rem(index + step, count)


def shards(
    queries,
    doc_of,
    doc_lengths,
    rotated_key_levels,
    rotated_value_levels,
    key_level_scale,
    value_level_scale,
):
    rows_home, width = queries.shape
    heads_dev = width // HEAD_WIDTH
    kv_dev = key_level_scale.shape[1]
    shard_len = rotated_key_levels.shape[1]
    n_doc = lax.axis_size("doc")
    n_ctx = lax.axis_size("ctx")
    n_head = lax.axis_size("head")
    cap = max(2, 3 * rows_home // (2 * n_doc))
    params = pltpu.CompilerParams(vmem_limit_bytes=VMEM_BYTES)
    vmem = pl.BlockSpec(memory_space=pltpu.VMEM)
    slots = heads_dev * cap
    slot_block = jax.ShapeDtypeStruct((slots, HEAD_WIDTH), jnp.bfloat16)

    key_block, value_block = rotated_key_levels[0], rotated_value_levels[0]
    args = (
        doc_of.reshape(1, rows_home),
        doc_lengths.reshape(1, doc_lengths.shape[0]),
        queries,
        key_block,
        value_block,
        key_level_scale[0],
        value_level_scale[0],
    )
    placing_block = jax.ShapeDtypeStruct((n_doc * (LANES // rows_home) * cap, LANES), jnp.bfloat16)
    hbm = pl.BlockSpec(memory_space=pltpu.HBM)
    anywhere = pl.BlockSpec(memory_space=pl.ANY)
    placing, shift, scales, own_key, own_value, *outgoing = pl.pallas_call(
        functools.partial(dispatch_kernel, n_doc, n_ctx, cap),
        out_shape=[
            placing_block,
            jax.ShapeDtypeStruct((n_ctx, shard_len), jnp.float32),
            jax.ShapeDtypeStruct((2 * kv_dev, shard_len), jnp.bfloat16),
            jax.ShapeDtypeStruct(key_block.shape, key_block.dtype),
            jax.ShapeDtypeStruct(value_block.shape, value_block.dtype),
        ]
        + [slot_block] * n_doc,
        in_specs=[hbm] * len(args),
        out_specs=[vmem] * (n_doc + 5),
        scratch_shapes=[
            pltpu.VMEM(args[at].shape, args[at].dtype) for at in (0, 1, 2, 5, 6)
        ]
        + [pltpu.SemaphoreType.DMA((len(args),))],
        compiler_params=params,
    )(*[pltpu.with_memory_space_constraint(arg, pltpu.HBM) for arg in args])
    cache = [own_key, own_value, scales]
    for step in range(1, n_ctx):
        pairs = [(i, (i + step) % n_ctx) for i in range(n_ctx)]
        cache += [lax.ppermute(part, "ctx", pairs) for part in (key_block, value_block, scales)]
    arrived = [outgoing[0]] + [sent(outgoing[k], "doc", k) for k in range(1, n_doc)]

    def attended_for(steps):
        sources = [arrived[k] for k in steps]
        rows = len(sources) * slots
        return pl.pallas_call(
            functools.partial(attend_kernel, len(sources), n_ctx, kv_dev),
            out_shape=[slot_block] * len(sources),
            in_specs=[vmem] * (1 + len(sources) + 3 * n_ctx),
            out_specs=[vmem] * len(sources),
            compiler_params=params,
            cost_estimate=pl.CostEstimate(
                flops=4 * rows * n_ctx * shard_len * HEAD_WIDTH,
                bytes_accessed=4 * n_ctx * shard_len * kv_dev * HEAD_WIDTH,
                transcendentals=rows * n_ctx * shard_len,
            ),
        )(shift, *sources, *cache)

    half = max(1, n_doc // 2)
    finished = []
    for first in range(0, n_doc, half):
        finished += attended_for(range(first, min(first + half, n_doc)))
    back = [finished[0]] + [returned(finished[k], "doc", k) for k in range(1, n_doc)]

    def assembled(pieces, before):
        return pl.pallas_call(
            functools.partial(assemble_kernel, n_head, [place for place, _ in pieces]),
            out_shape=jax.ShapeDtypeStruct((rows_home, n_head * width), jnp.bfloat16),
            in_specs=[anywhere] * len(pieces) + [hbm] * len(before),
            out_specs=hbm,
            scratch_shapes=[pltpu.SemaphoreType.DMA((len(pieces),))],
            input_output_aliases={len(pieces): 0} if before else {},
            compiler_params=params,
        )(*[block for _, block in pieces], *before)

    mine = pl.pallas_call(
        functools.partial(collect_kernel, n_doc, cap),
        out_shape=jax.ShapeDtypeStruct((rows_home, width), jnp.bfloat16),
        in_specs=[vmem] * (1 + n_doc),
        out_specs=vmem,
        compiler_params=params,
    )(placing, *back)

    if n_head != 4:
        return assembled(
            [((0, None), mine)]
            + [((step, None), returned(mine, "head", step)) for step in range(1, n_head)],
            (),
        )
    devices = [(c, h) for c in range(n_ctx) for h in range(n_head)]

    def swapped(value, step, parity):
        pairs = [
            (c * n_head + h, c * n_head + (h ^ step)) for c, h in devices if c % 2 == parity
        ]
        return lax.ppermute(value, ("ctx", "head"), pairs)

    mirror = returned(mine, "head", 3)
    near = returned(mine, "head", 1)
    second = swapped(mine, 2, 0)
    passed = swapped(mirror, 1, 1)
    attended = assembled([((0, None), mine), ((3, None), mirror)], ())
    return assembled([((1, None), near), ((2, 0), second), ((2, 1), passed)], (attended,))


def solution(mesh):
    in_specs = (
        P(("doc", "ctx"), "head"),
        P(("doc", "ctx"), None),
        P(),
        P("doc", "ctx", "head"),
        P("doc", "ctx", "head"),
        P("doc", "head", "ctx"),
        P("doc", "head", "ctx"),
    )
    out_specs = P(("doc", "ctx"), None)
    return jax.shard_map(shards, mesh=mesh, in_specs=in_specs, out_specs=out_specs, check_vma=False)
```

```python
import functools
import math

import jax
import jax.numpy as jnp
from jax import lax
from jax.experimental import pallas as pl
from jax.experimental.pallas import tpu as pltpu
from jax.sharding import PartitionSpec as P

HEAD_WIDTH = 128
LANES = 128
VMEM_BYTES = 40 * 1024 * 1024


def peer_of(index, step, count):
    if count & (count - 1) == 0:
        return index ^ step
    return (index + step) % count


def sent(value, axis, step):
    count = lax.axis_size(axis)
    return lax.ppermute(value, axis, [(i, peer_of(i, step, count)) for i in range(count)])


def returned(value, axis, step):
    count = lax.axis_size(axis)
    return lax.ppermute(value, axis, [(peer_of(i, step, count), i) for i in range(count)])


def sign_matrix():
    row = lax.broadcasted_iota(jnp.int32, (HEAD_WIDTH, HEAD_WIDTH), 0)
    column = lax.broadcasted_iota(jnp.int32, (HEAD_WIDTH, HEAD_WIDTH), 1)
    both = row & column
    both = both ^ (both >> 4)
    both = both ^ (both >> 2)
    both = both ^ (both >> 1)
    return (1 - 2 * (both & 1)).astype(jnp.float32).astype(jnp.bfloat16)


def placing_matrix(doc_row, n_doc, cap):
    rows = doc_row.shape[1]
    group = LANES // rows
    me = lax.axis_index("doc")
    square = (rows, rows)
    diagonal = lax.broadcasted_iota(jnp.int32, square, 0) == lax.broadcasted_iota(
        jnp.int32, square, 1
    )
    doc_column = jnp.sum(
        jnp.where(diagonal, jnp.broadcast_to(doc_row, square), 0), axis=1, keepdims=True
    )
    request = lax.broadcasted_iota(jnp.int32, (rows, LANES), 0)
    lane = lax.broadcasted_iota(jnp.int32, (rows, LANES), 1)
    docs = jnp.broadcast_to(doc_column, (rows, LANES))
    lane_request = lane % rows
    lane_doc = jnp.sum(jnp.where(request == lane_request, docs, 0), axis=0, keepdims=True)
    rank = jnp.sum(
        jnp.where((docs == lane_doc) & (request < lane_request), 1, 0), axis=0, keepdims=True
    )
    if n_doc & (n_doc - 1) == 0:
        step = lane_doc ^ me
    else:
        step = (lane_doc - me + n_doc) % n_doc
    place = step * (group * cap) + (lane[:1] // rows) * cap + rank
    slots = n_doc * group * cap
    slot = lax.broadcasted_iota(jnp.int32, (slots, LANES), 0)
    return jnp.where(slot == place, 1.0, 0.0).astype(jnp.bfloat16)


def dispatch_kernel(
    n_doc,
    n_ctx,
    cap,
    doc_hbm,
    length_hbm,
    query_hbm,
    key_hbm,
    value_hbm,
    key_scale_hbm,
    value_scale_hbm,
    placing_ref,
    shift_ref,
    cache_ref,
    *refs,
):
    out_refs, (doc_ref, length_ref, query_ref, key_scale_ref, value_scale_ref, sems) = (
        refs[:n_doc],
        refs[n_doc:],
    )
    shard_len, span = key_hbm.shape
    pairs = (
        (doc_hbm, doc_ref),
        (query_hbm, query_ref),
        (length_hbm, length_ref),
        (key_scale_hbm, key_scale_ref),
        (value_scale_hbm, value_scale_ref),
        (key_hbm, cache_ref.at[pl.ds(0, shard_len)]),
        (value_hbm, cache_ref.at[pl.ds(shard_len, shard_len)]),
    )
    copies = [
        pltpu.make_async_copy(source, target, sems.at[at])
        for at, (source, target) in enumerate(pairs)
    ]
    for copy in copies:
        copy.start()
    rows, width = query_ref.shape
    group = LANES // rows
    heads = width // HEAD_WIDTH
    block = group * cap
    signs = sign_matrix()
    scale = 1.0 / math.sqrt(HEAD_WIDTH)
    copies[0].wait()
    placing = placing_matrix(doc_ref[...], n_doc, cap)
    placing_ref[...] = placing
    copies[1].wait()
    rotated = []
    for g in range(heads // group):
        stacked = jnp.concatenate(
            [
                query_ref[:, (g * group + h) * HEAD_WIDTH : (g * group + h + 1) * HEAD_WIDTH]
                for h in range(group)
            ],
            axis=0,
        )
        product = jnp.dot(stacked, signs, preferred_element_type=jnp.float32) * scale
        rotated.append(product.astype(jnp.bfloat16))
    for g in range(heads // group):
        placed = jnp.dot(placing, rotated[g], preferred_element_type=jnp.float32).astype(
            jnp.bfloat16
        )
        for k in range(n_doc):
            out_refs[k][g * block : (g + 1) * block, :] = placed[k * block : (k + 1) * block]
    for copy in copies[2:5]:
        copy.wait()
    scale_rows = []
    for scale_ref in (key_scale_ref, value_scale_ref):
        scales = scale_ref[...].astype(jnp.float32)
        scale_rows += [
            scales[row : row + 1, at : at + span]
            for row in range(scales.shape[0])
            for at in range(0, shard_len, span)
        ]
    cache_ref[2 * shard_len :, :] = jnp.concatenate(scale_rows, axis=0).astype(jnp.bfloat16)
    lengths = length_ref[...]
    lane = lax.broadcasted_iota(jnp.int32, lengths.shape, 1)
    length = jnp.sum(
        jnp.where(lane == lax.axis_index("doc"), lengths, 0), axis=1, keepdims=True
    )
    step = lax.broadcasted_iota(jnp.int32, shift_ref.shape, 0)
    anchor = (lax.axis_index("ctx") - step + n_ctx) % n_ctx
    position = lax.broadcasted_iota(jnp.int32, shift_ref.shape, 1) + anchor * shard_len
    shift_ref[...] = jnp.where(position < length, 0.0, -1e30)
    for copy in copies[5:]:
        copy.wait()


def collect_kernel(n_doc, cap, placing_ref, *refs):
    back_refs, out_ref = refs[:n_doc], refs[n_doc]
    rows, width = out_ref.shape
    group = LANES // rows
    heads = width // HEAD_WIDTH
    block = group * cap
    placing = placing_ref[...]
    for g in range(heads // group):
        slots = jnp.concatenate(
            [back_refs[k][g * block : (g + 1) * block, :] for k in range(n_doc)], axis=0
        )
        mine = lax.dot_general(
            placing, slots, (((0,), (0,)), ((), ())), preferred_element_type=jnp.float32
        ).astype(jnp.bfloat16)
        for h in range(group):
            at = (g * group + h) * HEAD_WIDTH
            out_ref[:, at : at + HEAD_WIDTH] = mine[h * rows : (h + 1) * rows]


def attend_kernel(sources, n_ctx, kv_dev, shift_ref, *refs):
    query_refs, refs = refs[:sources], refs[sources:]
    cache_refs, out_refs = refs[:n_ctx], refs[n_ctx:]
    shard_len = shift_ref.shape[1]
    span = kv_dev * HEAD_WIDTH
    pieces = shard_len // span

    def scale_row(scales, row):
        return jnp.concatenate(
            [scales[row * pieces + at : row * pieces + at + 1, :] for at in range(pieces)], axis=1
        )

    rows_doc = query_refs[0].shape[0] // kv_dev
    signs = sign_matrix()
    scale = 1.0 / math.sqrt(HEAD_WIDTH)
    groups = range(kv_dev)
    spans = [slice(g * rows_doc, (g + 1) * rows_doc) for g in groups]
    heads = [slice(g * HEAD_WIDTH, (g + 1) * HEAD_WIDTH) for g in groups]
    rows = [jnp.concatenate([ref[span, :] for ref in query_refs], axis=0) for span in spans]
    states = [None] * kv_dev
    for first in range(0, n_ctx, 2):
        steps = range(first, min(first + 2, n_ctx))
        scales = {step: cache_refs[step][2 * shard_len :, :].astype(jnp.float32) for step in steps}
        scores = {}
        for g in groups:
            for step in steps:
                key_scale = scale_row(scales[step], g) * (scale * math.log2(math.e))
                product = lax.dot_general(
                    rows[g],
                    cache_refs[step][:shard_len, heads[g]],
                    (((1,), (1,)), ((), ())),
                    preferred_element_type=jnp.float32,
                )
                scores[g, step] = product * key_scale + shift_ref[step : step + 1, :]
        tops = []
        for g in groups:
            top = functools.reduce(
                jnp.maximum, [jnp.max(scores[g, step], axis=-1, keepdims=True) for step in steps]
            )
            tops.append(top if states[g] is None else jnp.maximum(top, states[g][0]))
        for g in groups:
            all_probs, summed = 0.0, 0.0
            for step in steps:
                value_scale = scale_row(scales[step], kv_dev + g)
                probs = jnp.exp2(scores[g, step] - tops[g])
                all_probs = all_probs + probs
                weights = (probs * value_scale).astype(jnp.bfloat16)
                summed = summed + jnp.dot(
                    weights,
                    cache_refs[step][shard_len : 2 * shard_len, heads[g]],
                    preferred_element_type=jnp.float32,
                )
            total = jnp.sum(all_probs, axis=-1, keepdims=True)
            if states[g] is not None:
                factor = jnp.exp2(states[g][0] - tops[g])
                total = total + states[g][1] * factor
                summed = summed + states[g][2] * factor
            states[g] = (tops[g], total, summed)
    for g in groups:
        _, total, summed = states[g]
        mixed = summed * (scale / total)
        high = mixed.astype(jnp.bfloat16)
        low = (mixed - high.astype(jnp.float32)).astype(jnp.bfloat16)
        result = jnp.dot(high, signs, preferred_element_type=jnp.float32) + jnp.dot(
            low, signs, preferred_element_type=jnp.float32
        )
        result = result.astype(jnp.bfloat16)
        for k in range(sources):
            out_refs[k][spans[g], :] = result[k * rows_doc : (k + 1) * rows_doc]


def assemble_kernel(n_head, places, *refs):
    block_refs, out_ref, sems = refs[: len(places)], refs[-2], refs[-1]
    me, parity = lax.axis_index("head"), lax.rem(lax.axis_index("ctx"), 2)
    width = block_refs[0].shape[1]
    copies = []
    for at, (even, odd) in enumerate(places):
        step = jnp.where(parity == 0, even or 0, odd or 0)
        column = pl.multiple_of(peer_of_traced(me, step, n_head) * width, width)
        copy = pltpu.make_async_copy(
            block_refs[at], out_ref.at[:, pl.ds(column, width)], sems.at[at]
        )
        copies.append((copy, 1 if even is None else 0 if odd is None else None))
    for copy, wanted in copies:
        if wanted is None:
            copy.start()
        else:
            pl.when(parity == wanted)(copy.start)
    for copy, wanted in copies:
        if wanted is None:
            copy.wait()
        else:
            pl.when(parity == wanted)(copy.wait)


def peer_of_traced(index, step, count):
    if count & (count - 1) == 0:
        return index ^ step
    return lax.rem(index + step, count)


def shards(
    queries,
    doc_of,
    doc_lengths,
    rotated_key_levels,
    rotated_value_levels,
    key_level_scale,
    value_level_scale,
):
    rows_home, width = queries.shape
    heads_dev = width // HEAD_WIDTH
    kv_dev = key_level_scale.shape[1]
    shard_len = rotated_key_levels.shape[1]
    n_doc = lax.axis_size("doc")
    n_ctx = lax.axis_size("ctx")
    n_head = lax.axis_size("head")
    cap = max(2, 3 * rows_home // (2 * n_doc))
    params = pltpu.CompilerParams(vmem_limit_bytes=VMEM_BYTES)
    vmem = pl.BlockSpec(memory_space=pltpu.VMEM)
    slots = heads_dev * cap
    slot_block = jax.ShapeDtypeStruct((slots, HEAD_WIDTH), jnp.bfloat16)

    key_block, value_block = rotated_key_levels[0], rotated_value_levels[0]
    args = (
        doc_of.reshape(1, rows_home),
        doc_lengths.reshape(1, doc_lengths.shape[0]),
        queries,
        key_block,
        value_block,
        key_level_scale[0],
        value_level_scale[0],
    )
    placing_block = jax.ShapeDtypeStruct((n_doc * (LANES // rows_home) * cap, LANES), jnp.bfloat16)
    hbm = pl.BlockSpec(memory_space=pltpu.HBM)
    anywhere = pl.BlockSpec(memory_space=pl.ANY)
    cache_rows = 2 * shard_len + 2 * shard_len // HEAD_WIDTH
    placing, shift, own_cache, *outgoing = pl.pallas_call(
        functools.partial(dispatch_kernel, n_doc, n_ctx, cap),
        out_shape=[
            placing_block,
            jax.ShapeDtypeStruct((n_ctx, shard_len), jnp.float32),
            jax.ShapeDtypeStruct((cache_rows, kv_dev * HEAD_WIDTH), key_block.dtype),
        ]
        + [slot_block] * n_doc,
        in_specs=[hbm] * len(args),
        out_specs=[vmem] * (n_doc + 3),
        scratch_shapes=[
            pltpu.VMEM(args[at].shape, args[at].dtype) for at in (0, 1, 2, 5, 6)
        ]
        + [pltpu.SemaphoreType.DMA((len(args),))],
        compiler_params=params,
    )(*[pltpu.with_memory_space_constraint(arg, pltpu.HBM) for arg in args])
    cache = [own_cache]
    for step in range(1, n_ctx):
        cache.append(
            lax.ppermute(own_cache, "ctx", [(i, (i + step) % n_ctx) for i in range(n_ctx)])
        )
    arrived = [outgoing[0]] + [sent(outgoing[k], "doc", k) for k in range(1, n_doc)]

    def attended_for(steps, shift):
        sources = [arrived[k] for k in steps]
        rows = len(sources) * slots
        return pl.pallas_call(
            functools.partial(attend_kernel, len(sources), n_ctx, kv_dev),
            out_shape=[slot_block] * len(sources),
            in_specs=[vmem] * (1 + len(sources) + n_ctx),
            out_specs=[vmem] * len(sources),
            compiler_params=params,
            cost_estimate=pl.CostEstimate(
                flops=4 * rows * n_ctx * shard_len * HEAD_WIDTH,
                bytes_accessed=4 * n_ctx * shard_len * kv_dev * HEAD_WIDTH,
                transcendentals=rows * n_ctx * shard_len,
            ),
        )(shift, *sources, *cache)

    half = max(1, n_doc // 2)
    finished = []
    for first in range(0, n_doc, half):
        finished += attended_for(range(first, min(first + half, n_doc)), shift)
        finished[0], shift = lax.optimization_barrier((finished[0], shift))
    back = [finished[0]] + [returned(finished[k], "doc", k) for k in range(1, n_doc)]

    def assembled(pieces, before):
        return pl.pallas_call(
            functools.partial(assemble_kernel, n_head, [place for place, _ in pieces]),
            out_shape=jax.ShapeDtypeStruct((rows_home, n_head * width), jnp.bfloat16),
            in_specs=[anywhere] * len(pieces) + [hbm] * len(before),
            out_specs=hbm,
            scratch_shapes=[pltpu.SemaphoreType.DMA((len(pieces),))],
            input_output_aliases={len(pieces): 0} if before else {},
            compiler_params=params,
        )(*[block for _, block in pieces], *before)

    mine = pl.pallas_call(
        functools.partial(collect_kernel, n_doc, cap),
        out_shape=jax.ShapeDtypeStruct((rows_home, width), jnp.bfloat16),
        in_specs=[vmem] * (1 + n_doc),
        out_specs=vmem,
        compiler_params=params,
    )(placing, *back)

    if n_head != 4:
        return assembled(
            [((0, 0), mine)]
            + [((step, step), returned(mine, "head", step)) for step in range(1, n_head)],
            (),
        )

    def swapped(value, even, odd):
        pairs = []
        for c in range(n_ctx):
            step = odd if c % 2 else even
            if step is not None:
                pairs += [(c * n_head + h, c * n_head + (h ^ step)) for h in range(n_head)]
        return lax.ppermute(value, ("ctx", "head"), pairs)

    first = swapped(mine, 3, 3)
    second = swapped(mine, 1, 1)
    third = swapped(mine, 2, None)
    passed = swapped(first, None, 1)
    attended = assembled([((0, 0), mine), ((3, 3), first)], ())
    return assembled(
        [((2, None), third), ((1, 1), second), ((None, 2), passed)], (attended,)
    )


def solution(mesh):
    in_specs = (
        P(("doc", "ctx"), "head"),
        P(("doc", "ctx"), None),
        P(),
        P("doc", "ctx", "head"),
        P("doc", "ctx", "head"),
        P("doc", "head", "ctx"),
        P("doc", "head", "ctx"),
    )
    out_specs = P(("doc", "ctx"), None)
    return jax.shard_map(shards, mesh=mesh, in_specs=in_specs, out_specs=out_specs, check_vma=False)
```

```python
import functools
import math

import jax
import jax.numpy as jnp
from jax import lax
from jax.experimental import pallas as pl
from jax.experimental.pallas import tpu as pltpu
from jax.sharding import PartitionSpec as P

HEAD_WIDTH = 128
LANES = 128
VMEM_BYTES = 40 * 1024 * 1024


def peer_of(index, step, count):
    if count & (count - 1) == 0:
        return index ^ step
    return (index + step) % count


def sent(value, axis, step):
    count = lax.axis_size(axis)
    return lax.ppermute(value, axis, [(i, peer_of(i, step, count)) for i in range(count)])


def returned(value, axis, step):
    count = lax.axis_size(axis)
    return lax.ppermute(value, axis, [(peer_of(i, step, count), i) for i in range(count)])


def sign_matrix():
    row = lax.broadcasted_iota(jnp.int32, (HEAD_WIDTH, HEAD_WIDTH), 0)
    column = lax.broadcasted_iota(jnp.int32, (HEAD_WIDTH, HEAD_WIDTH), 1)
    both = row & column
    both = both ^ (both >> 4)
    both = both ^ (both >> 2)
    both = both ^ (both >> 1)
    return (1 - 2 * (both & 1)).astype(jnp.float32).astype(jnp.bfloat16)


def placing_matrix(doc_row, n_doc, cap):
    rows = doc_row.shape[1]
    group = LANES // rows
    me = lax.axis_index("doc")
    square = (rows, rows)
    diagonal = lax.broadcasted_iota(jnp.int32, square, 0) == lax.broadcasted_iota(
        jnp.int32, square, 1
    )
    doc_column = jnp.sum(
        jnp.where(diagonal, jnp.broadcast_to(doc_row, square), 0), axis=1, keepdims=True
    )
    request = lax.broadcasted_iota(jnp.int32, (rows, LANES), 0)
    lane = lax.broadcasted_iota(jnp.int32, (rows, LANES), 1)
    docs = jnp.broadcast_to(doc_column, (rows, LANES))
    lane_request = lane % rows
    lane_doc = jnp.sum(jnp.where(request == lane_request, docs, 0), axis=0, keepdims=True)
    rank = jnp.sum(
        jnp.where((docs == lane_doc) & (request < lane_request), 1, 0), axis=0, keepdims=True
    )
    if n_doc & (n_doc - 1) == 0:
        step = lane_doc ^ me
    else:
        step = (lane_doc - me + n_doc) % n_doc
    place = step * (group * cap) + (lane[:1] // rows) * cap + rank
    slots = n_doc * group * cap
    slot = lax.broadcasted_iota(jnp.int32, (slots, LANES), 0)
    return jnp.where(slot == place, 1.0, 0.0).astype(jnp.bfloat16)


def dispatch_kernel(
    n_doc,
    n_ctx,
    cap,
    doc_hbm,
    length_hbm,
    query_hbm,
    key_hbm,
    value_hbm,
    key_scale_hbm,
    value_scale_hbm,
    placing_ref,
    valid_ref,
    cache_ref,
    *refs,
):
    out_refs, (doc_ref, length_ref, query_ref, key_scale_ref, value_scale_ref, sems) = (
        refs[:n_doc],
        refs[n_doc:],
    )
    shard_len, span = key_hbm.shape
    pairs = (
        (doc_hbm, doc_ref),
        (query_hbm, query_ref),
        (length_hbm, length_ref),
        (key_scale_hbm, key_scale_ref),
        (value_scale_hbm, value_scale_ref),
        (key_hbm, cache_ref.at[pl.ds(0, shard_len)]),
        (value_hbm, cache_ref.at[pl.ds(shard_len, shard_len)]),
    )
    copies = [
        pltpu.make_async_copy(source, target, sems.at[at])
        for at, (source, target) in enumerate(pairs)
    ]
    for copy in copies:
        copy.start()
    rows, width = query_ref.shape
    group = LANES // rows
    heads = width // HEAD_WIDTH
    block = group * cap
    signs = sign_matrix()
    scale = 1.0 / math.sqrt(HEAD_WIDTH)
    copies[0].wait()
    placing = placing_matrix(doc_ref[...], n_doc, cap)
    placing_ref[...] = placing
    copies[1].wait()
    rotated = []
    for g in range(heads // group):
        stacked = jnp.concatenate(
            [
                query_ref[:, (g * group + h) * HEAD_WIDTH : (g * group + h + 1) * HEAD_WIDTH]
                for h in range(group)
            ],
            axis=0,
        )
        product = jnp.dot(stacked, signs, preferred_element_type=jnp.float32) * scale
        rotated.append(product.astype(jnp.bfloat16))
    for g in range(heads // group):
        placed = jnp.dot(placing, rotated[g], preferred_element_type=jnp.float32).astype(
            jnp.bfloat16
        )
        for k in range(n_doc):
            out_refs[k][g * block : (g + 1) * block, :] = placed[k * block : (k + 1) * block]
    for copy in copies[2:5]:
        copy.wait()
    scale_rows = []
    for scale_ref in (key_scale_ref, value_scale_ref):
        scales = scale_ref[...].astype(jnp.float32)
        scale_rows += [
            scales[row : row + 1, at : at + span]
            for row in range(scales.shape[0])
            for at in range(0, shard_len, span)
        ]
    cache_ref[2 * shard_len :, :] = jnp.concatenate(scale_rows, axis=0).astype(jnp.bfloat16)
    lengths = length_ref[...]
    lane = lax.broadcasted_iota(jnp.int32, lengths.shape, 1)
    length = jnp.sum(
        jnp.where(lane == lax.axis_index("doc"), lengths, 0), axis=1, keepdims=True
    )
    step = lax.broadcasted_iota(jnp.int32, valid_ref.shape, 0)
    anchor = (lax.axis_index("ctx") - step + n_ctx) % n_ctx
    position = lax.broadcasted_iota(jnp.int32, valid_ref.shape, 1) + anchor * shard_len
    valid_ref[...] = jnp.where(position < length, 1.0, 0.0)
    for copy in copies[5:]:
        copy.wait()


def collect_kernel(n_doc, cap, placing_ref, *refs):
    back_refs, out_ref = refs[:n_doc], refs[n_doc]
    rows, width = out_ref.shape
    group = LANES // rows
    heads = width // HEAD_WIDTH
    block = group * cap
    placing = placing_ref[...]
    for g in range(heads // group):
        slots = jnp.concatenate(
            [back_refs[k][g * block : (g + 1) * block, :] for k in range(n_doc)], axis=0
        )
        mine = lax.dot_general(
            placing, slots, (((0,), (0,)), ((), ())), preferred_element_type=jnp.float32
        ).astype(jnp.bfloat16)
        for h in range(group):
            at = (g * group + h) * HEAD_WIDTH
            out_ref[:, at : at + HEAD_WIDTH] = mine[h * rows : (h + 1) * rows]


def attend_kernel(sources, n_ctx, kv_dev, valid_ref, *refs):
    query_refs, refs = refs[:sources], refs[sources:]
    cache_refs, out_refs = refs[:n_ctx], refs[n_ctx:]
    shard_len = valid_ref.shape[1]
    span = kv_dev * HEAD_WIDTH
    pieces = shard_len // span

    def scale_row(scales, row):
        return jnp.concatenate(
            [scales[row * pieces + at : row * pieces + at + 1, :] for at in range(pieces)], axis=1
        )

    rows_doc = query_refs[0].shape[0] // kv_dev
    signs = sign_matrix()
    scale = 1.0 / math.sqrt(HEAD_WIDTH)
    groups = range(kv_dev)
    spans = [slice(g * rows_doc, (g + 1) * rows_doc) for g in groups]
    heads = [slice(g * HEAD_WIDTH, (g + 1) * HEAD_WIDTH) for g in groups]
    rows = [jnp.concatenate([ref[span, :] for ref in query_refs], axis=0) for span in spans]
    states = [None] * kv_dev
    for first in range(0, n_ctx, 2):
        steps = range(first, min(first + 2, n_ctx))
        scales = {step: cache_refs[step][2 * shard_len :, :].astype(jnp.float32) for step in steps}
        valid = {step: valid_ref[step : step + 1, :] > 0.0 for step in steps}
        scores = {}
        for g in groups:
            for step in steps:
                key_scale = scale_row(scales[step], g) * (scale * math.log2(math.e))
                product = lax.dot_general(
                    rows[g],
                    cache_refs[step][:shard_len, heads[g]],
                    (((1,), (1,)), ((), ())),
                    preferred_element_type=jnp.float32,
                )
                scores[g, step] = jnp.where(valid[step], product * key_scale, -1e30)
        tops = []
        for g in groups:
            top = functools.reduce(
                jnp.maximum, [jnp.max(scores[g, step], axis=-1, keepdims=True) for step in steps]
            )
            tops.append(top if states[g] is None else jnp.maximum(top, states[g][0]))
        for g in groups:
            all_probs, summed = 0.0, 0.0
            for step in steps:
                value_scale = scale_row(scales[step], kv_dev + g)
                probs = jnp.exp2(scores[g, step] - tops[g])
                all_probs = all_probs + probs
                weights = (probs * value_scale).astype(jnp.bfloat16)
                summed = summed + jnp.dot(
                    weights,
                    cache_refs[step][shard_len : 2 * shard_len, heads[g]],
                    preferred_element_type=jnp.float32,
                )
            total = jnp.sum(all_probs, axis=-1, keepdims=True)
            if states[g] is not None:
                factor = jnp.exp2(states[g][0] - tops[g])
                total = total + states[g][1] * factor
                summed = summed + states[g][2] * factor
            states[g] = (tops[g], total, summed)
    for g in groups:
        _, total, summed = states[g]
        mixed = summed * (scale / total)
        high = mixed.astype(jnp.bfloat16)
        low = (mixed - high.astype(jnp.float32)).astype(jnp.bfloat16)
        result = jnp.dot(high, signs, preferred_element_type=jnp.float32) + jnp.dot(
            low, signs, preferred_element_type=jnp.float32
        )
        result = result.astype(jnp.bfloat16)
        for k in range(sources):
            out_refs[k][spans[g], :] = result[k * rows_doc : (k + 1) * rows_doc]


def assemble_kernel(n_head, places, *refs):
    block_refs, out_ref, sems = refs[: len(places)], refs[-2], refs[-1]
    me, parity = lax.axis_index("head"), lax.rem(lax.axis_index("ctx"), 2)
    width = block_refs[0].shape[1]
    copies = []
    for at, (even, odd) in enumerate(places):
        step = jnp.where(parity == 0, even or 0, odd or 0)
        column = pl.multiple_of(peer_of_traced(me, step, n_head) * width, width)
        copy = pltpu.make_async_copy(
            block_refs[at], out_ref.at[:, pl.ds(column, width)], sems.at[at]
        )
        copies.append((copy, 1 if even is None else 0 if odd is None else None))
    for copy, wanted in copies:
        if wanted is None:
            copy.start()
        else:
            pl.when(parity == wanted)(copy.start)
    for copy, wanted in copies:
        if wanted is None:
            copy.wait()
        else:
            pl.when(parity == wanted)(copy.wait)


def peer_of_traced(index, step, count):
    if count & (count - 1) == 0:
        return index ^ step
    return lax.rem(index + step, count)


def shards(
    queries,
    doc_of,
    doc_lengths,
    rotated_key_levels,
    rotated_value_levels,
    key_level_scale,
    value_level_scale,
):
    rows_home, width = queries.shape
    heads_dev = width // HEAD_WIDTH
    kv_dev = key_level_scale.shape[1]
    shard_len = rotated_key_levels.shape[1]
    n_doc = lax.axis_size("doc")
    n_ctx = lax.axis_size("ctx")
    n_head = lax.axis_size("head")
    cap = max(2, 3 * rows_home // (2 * n_doc))
    params = pltpu.CompilerParams(vmem_limit_bytes=VMEM_BYTES)
    vmem = pl.BlockSpec(memory_space=pltpu.VMEM)
    slots = heads_dev * cap
    slot_block = jax.ShapeDtypeStruct((slots, HEAD_WIDTH), jnp.bfloat16)

    key_block, value_block = rotated_key_levels[0], rotated_value_levels[0]
    args = (
        doc_of.reshape(1, rows_home),
        doc_lengths.reshape(1, doc_lengths.shape[0]),
        queries,
        key_block,
        value_block,
        key_level_scale[0],
        value_level_scale[0],
    )
    placing_block = jax.ShapeDtypeStruct((n_doc * (LANES // rows_home) * cap, LANES), jnp.bfloat16)
    hbm = pl.BlockSpec(memory_space=pltpu.HBM)
    anywhere = pl.BlockSpec(memory_space=pl.ANY)
    cache_rows = 2 * shard_len + 2 * shard_len // HEAD_WIDTH
    placing, valid, own_cache, *outgoing = pl.pallas_call(
        functools.partial(dispatch_kernel, n_doc, n_ctx, cap),
        out_shape=[
            placing_block,
            jax.ShapeDtypeStruct((n_ctx, shard_len), jnp.float32),
            jax.ShapeDtypeStruct((cache_rows, kv_dev * HEAD_WIDTH), key_block.dtype),
        ]
        + [slot_block] * n_doc,
        in_specs=[hbm] * len(args),
        out_specs=[vmem] * (n_doc + 3),
        scratch_shapes=[
            pltpu.VMEM(args[at].shape, args[at].dtype) for at in (0, 1, 2, 5, 6)
        ]
        + [pltpu.SemaphoreType.DMA((len(args),))],
        compiler_params=params,
    )(*[pltpu.with_memory_space_constraint(arg, pltpu.HBM) for arg in args])
    cache = [own_cache]
    for step in range(1, n_ctx):
        cache.append(
            lax.ppermute(own_cache, "ctx", [(i, (i + step) % n_ctx) for i in range(n_ctx)])
        )
    arrived = [outgoing[0]] + [sent(outgoing[k], "doc", k) for k in range(1, n_doc)]

    def attended_for(steps, valid):
        sources = [arrived[k] for k in steps]
        rows = len(sources) * slots
        return pl.pallas_call(
            functools.partial(attend_kernel, len(sources), n_ctx, kv_dev),
            out_shape=[slot_block] * len(sources),
            in_specs=[vmem] * (1 + len(sources) + n_ctx),
            out_specs=[vmem] * len(sources),
            compiler_params=params,
            cost_estimate=pl.CostEstimate(
                flops=4 * rows * n_ctx * shard_len * HEAD_WIDTH,
                bytes_accessed=4 * n_ctx * shard_len * kv_dev * HEAD_WIDTH,
                transcendentals=rows * n_ctx * shard_len,
            ),
        )(valid, *sources, *cache)

    finished = {}
    for steps in (range(1, n_doc - 1), range(max(1, n_doc - 1), n_doc)):
        if len(steps) > 0:
            finished.update(zip(steps, attended_for(steps, valid)))
    if n_doc > 1:
        finished[n_doc - 1], valid = lax.optimization_barrier((finished[n_doc - 1], valid))
    finished[0] = attended_for((0,), valid)[0]
    back = [finished[0]] + [returned(finished[k], "doc", k) for k in range(1, n_doc)]

    def assembled(pieces, before):
        return pl.pallas_call(
            functools.partial(assemble_kernel, n_head, [place for place, _ in pieces]),
            out_shape=jax.ShapeDtypeStruct((rows_home, n_head * width), jnp.bfloat16),
            in_specs=[anywhere] * len(pieces) + [hbm] * len(before),
            out_specs=hbm,
            scratch_shapes=[pltpu.SemaphoreType.DMA((len(pieces),))],
            input_output_aliases={len(pieces): 0} if before else {},
            compiler_params=params,
        )(*[block for _, block in pieces], *before)

    mine = pl.pallas_call(
        functools.partial(collect_kernel, n_doc, cap),
        out_shape=jax.ShapeDtypeStruct((rows_home, width), jnp.bfloat16),
        in_specs=[vmem] * (1 + n_doc),
        out_specs=vmem,
        compiler_params=params,
    )(placing, *back)

    if n_head != 4:
        return assembled(
            [((0, 0), mine)]
            + [((step, step), returned(mine, "head", step)) for step in range(1, n_head)],
            (),
        )

    def swapped(value, even, odd):
        pairs = []
        for c in range(n_ctx):
            step = odd if c % 2 else even
            if step is not None:
                pairs += [(c * n_head + h, c * n_head + (h ^ step)) for h in range(n_head)]
        return lax.ppermute(value, ("ctx", "head"), pairs)

    first = swapped(mine, 3, 3)
    second = swapped(mine, 1, 1)
    third = swapped(mine, 2, None)
    passed = swapped(first, None, 1)
    attended = assembled([((0, 0), mine), ((3, 3), first)], ())
    return assembled(
        [((2, None), third), ((1, 1), second), ((None, 2), passed)], (attended,)
    )


def solution(mesh):
    in_specs = (
        P(("doc", "ctx"), "head"),
        P(("doc", "ctx"), None),
        P(),
        P("doc", "ctx", "head"),
        P("doc", "ctx", "head"),
        P("doc", "head", "ctx"),
        P("doc", "head", "ctx"),
    )
    out_specs = P(("doc", "ctx"), None)
    return jax.shard_map(shards, mesh=mesh, in_specs=in_specs, out_specs=out_specs, check_vma=False)
```

```python
import functools
import math

import jax
import jax.numpy as jnp
from jax import lax
from jax.experimental import pallas as pl
from jax.experimental.pallas import tpu as pltpu
from jax.sharding import PartitionSpec as P

HEAD_WIDTH = 128
LANES = 128
VMEM_BYTES = 40 * 1024 * 1024


def peer_of(index, step, count):
    if count & (count - 1) == 0:
        return index ^ step
    return (index + step) % count


def sent(value, axis, step):
    count = lax.axis_size(axis)
    return lax.ppermute(value, axis, [(i, peer_of(i, step, count)) for i in range(count)])


def returned(value, axis, step):
    count = lax.axis_size(axis)
    return lax.ppermute(value, axis, [(peer_of(i, step, count), i) for i in range(count)])


def sign_matrix():
    row = lax.broadcasted_iota(jnp.int32, (HEAD_WIDTH, HEAD_WIDTH), 0)
    column = lax.broadcasted_iota(jnp.int32, (HEAD_WIDTH, HEAD_WIDTH), 1)
    both = row & column
    both = both ^ (both >> 4)
    both = both ^ (both >> 2)
    both = both ^ (both >> 1)
    return (1 - 2 * (both & 1)).astype(jnp.float32).astype(jnp.bfloat16)


def placing_matrix(doc_row, n_doc, cap):
    rows = doc_row.shape[1]
    group = LANES // rows
    me = lax.axis_index("doc")
    square = (rows, rows)
    diagonal = lax.broadcasted_iota(jnp.int32, square, 0) == lax.broadcasted_iota(
        jnp.int32, square, 1
    )
    doc_column = jnp.sum(
        jnp.where(diagonal, jnp.broadcast_to(doc_row, square), 0), axis=1, keepdims=True
    )
    request = lax.broadcasted_iota(jnp.int32, (rows, LANES), 0)
    lane = lax.broadcasted_iota(jnp.int32, (rows, LANES), 1)
    docs = jnp.broadcast_to(doc_column, (rows, LANES))
    lane_request = lane % rows
    lane_doc = jnp.sum(jnp.where(request == lane_request, docs, 0), axis=0, keepdims=True)
    rank = jnp.sum(
        jnp.where((docs == lane_doc) & (request < lane_request), 1, 0), axis=0, keepdims=True
    )
    if n_doc & (n_doc - 1) == 0:
        step = lane_doc ^ me
    else:
        step = (lane_doc - me + n_doc) % n_doc
    place = step * (group * cap) + (lane[:1] // rows) * cap + rank
    slots = n_doc * group * cap
    slot = lax.broadcasted_iota(jnp.int32, (slots, LANES), 0)
    return jnp.where(slot == place, 1.0, 0.0).astype(jnp.bfloat16)


def dispatch_kernel(
    n_doc,
    n_ctx,
    cap,
    doc_hbm,
    length_hbm,
    query_hbm,
    key_hbm,
    value_hbm,
    key_scale_hbm,
    value_scale_hbm,
    placing_ref,
    valid_ref,
    cache_ref,
    *refs,
):
    out_refs, (doc_ref, length_ref, query_ref, key_scale_ref, value_scale_ref, sems) = (
        refs[:n_doc],
        refs[n_doc:],
    )
    shard_len, span = key_hbm.shape
    pairs = (
        (doc_hbm, doc_ref),
        (query_hbm, query_ref),
        (length_hbm, length_ref),
        (key_scale_hbm, key_scale_ref),
        (value_scale_hbm, value_scale_ref),
        (key_hbm, cache_ref.at[pl.ds(0, shard_len)]),
        (value_hbm, cache_ref.at[pl.ds(shard_len, shard_len)]),
    )
    copies = [
        pltpu.make_async_copy(source, target, sems.at[at])
        for at, (source, target) in enumerate(pairs)
    ]
    for copy in copies:
        copy.start()
    rows, width = query_ref.shape
    group = LANES // rows
    heads = width // HEAD_WIDTH
    block = group * cap
    signs = sign_matrix()
    scale = 1.0 / math.sqrt(HEAD_WIDTH)
    copies[0].wait()
    placing = placing_matrix(doc_ref[...], n_doc, cap)
    placing_ref[...] = placing
    copies[1].wait()
    rotated = []
    for g in range(heads // group):
        stacked = jnp.concatenate(
            [
                query_ref[:, (g * group + h) * HEAD_WIDTH : (g * group + h + 1) * HEAD_WIDTH]
                for h in range(group)
            ],
            axis=0,
        )
        product = jnp.dot(stacked, signs, preferred_element_type=jnp.float32) * scale
        rotated.append(product.astype(jnp.bfloat16))
    for g in range(heads // group):
        placed = jnp.dot(placing, rotated[g], preferred_element_type=jnp.float32).astype(
            jnp.bfloat16
        )
        for k in range(n_doc):
            out_refs[k][g * block : (g + 1) * block, :] = placed[k * block : (k + 1) * block]
    for copy in copies[2:5]:
        copy.wait()
    scale_rows = []
    for scale_ref in (key_scale_ref, value_scale_ref):
        scales = scale_ref[...].astype(jnp.float32)
        scale_rows += [
            scales[row : row + 1, at : at + span]
            for row in range(scales.shape[0])
            for at in range(0, shard_len, span)
        ]
    cache_ref[2 * shard_len :, :] = jnp.concatenate(scale_rows, axis=0).astype(jnp.bfloat16)
    lengths = length_ref[...]
    lane = lax.broadcasted_iota(jnp.int32, lengths.shape, 1)
    length = jnp.sum(
        jnp.where(lane == lax.axis_index("doc"), lengths, 0), axis=1, keepdims=True
    )
    step = lax.broadcasted_iota(jnp.int32, valid_ref.shape, 0)
    anchor = (lax.axis_index("ctx") - step + n_ctx) % n_ctx
    position = lax.broadcasted_iota(jnp.int32, valid_ref.shape, 1) + anchor * shard_len
    valid_ref[...] = jnp.where(position < length, 1.0, 0.0)
    for copy in copies[5:]:
        copy.wait()


def collect_kernel(n_doc, cap, placing_ref, *refs):
    back_refs, out_ref = refs[:n_doc], refs[n_doc]
    rows, width = out_ref.shape
    group = LANES // rows
    heads = width // HEAD_WIDTH
    block = group * cap
    placing = placing_ref[...]
    for g in range(heads // group):
        slots = jnp.concatenate(
            [back_refs[k][g * block : (g + 1) * block, :] for k in range(n_doc)], axis=0
        )
        mine = lax.dot_general(
            placing, slots, (((0,), (0,)), ((), ())), preferred_element_type=jnp.float32
        ).astype(jnp.bfloat16)
        for h in range(group):
            at = (g * group + h) * HEAD_WIDTH
            out_ref[:, at : at + HEAD_WIDTH] = mine[h * rows : (h + 1) * rows]


def attend_kernel(sources, n_ctx, kv_dev, valid_ref, *refs):
    query_refs, refs = refs[:sources], refs[sources:]
    cache_refs, out_refs = refs[:n_ctx], refs[n_ctx:]
    shard_len = valid_ref.shape[1]
    span = kv_dev * HEAD_WIDTH
    pieces = shard_len // span

    def scale_row(scales, row):
        return jnp.concatenate(
            [scales[row * pieces + at : row * pieces + at + 1, :] for at in range(pieces)], axis=1
        )

    rows_doc = query_refs[0].shape[0] // kv_dev
    signs = sign_matrix()
    scale = 1.0 / math.sqrt(HEAD_WIDTH)
    groups = range(kv_dev)
    spans = [slice(g * rows_doc, (g + 1) * rows_doc) for g in groups]
    heads = [slice(g * HEAD_WIDTH, (g + 1) * HEAD_WIDTH) for g in groups]
    rows = [jnp.concatenate([ref[span, :] for ref in query_refs], axis=0) for span in spans]
    states = [None] * kv_dev
    for first in range(0, n_ctx, 2):
        steps = range(first, min(first + 2, n_ctx))
        scales = {step: cache_refs[step][2 * shard_len :, :].astype(jnp.float32) for step in steps}
        valid = {step: valid_ref[step : step + 1, :] > 0.0 for step in steps}
        scores = {}
        for g in groups:
            for step in steps:
                key_scale = scale_row(scales[step], g) * (scale * math.log2(math.e))
                product = lax.dot_general(
                    rows[g],
                    cache_refs[step][:shard_len, heads[g]],
                    (((1,), (1,)), ((), ())),
                    preferred_element_type=jnp.float32,
                )
                scores[g, step] = jnp.where(valid[step], product * key_scale, -1e30)
        tops = []
        for g in groups:
            top = functools.reduce(
                jnp.maximum, [jnp.max(scores[g, step], axis=-1, keepdims=True) for step in steps]
            )
            tops.append(top if states[g] is None else jnp.maximum(top, states[g][0]))
        for g in groups:
            all_probs, summed = 0.0, 0.0
            for step in steps:
                value_scale = scale_row(scales[step], kv_dev + g)
                probs = jnp.exp2(scores[g, step] - tops[g])
                all_probs = all_probs + probs
                weights = (probs * value_scale).astype(jnp.bfloat16)
                summed = summed + jnp.dot(
                    weights,
                    cache_refs[step][shard_len : 2 * shard_len, heads[g]],
                    preferred_element_type=jnp.float32,
                )
            total = jnp.sum(all_probs, axis=-1, keepdims=True)
            if states[g] is not None:
                factor = jnp.exp2(states[g][0] - tops[g])
                total = total + states[g][1] * factor
                summed = summed + states[g][2] * factor
            states[g] = (tops[g], total, summed)
    for g in groups:
        _, total, summed = states[g]
        mixed = summed * (scale / total)
        high = mixed.astype(jnp.bfloat16)
        low = (mixed - high.astype(jnp.float32)).astype(jnp.bfloat16)
        result = jnp.dot(high, signs, preferred_element_type=jnp.float32) + jnp.dot(
            low, signs, preferred_element_type=jnp.float32
        )
        result = result.astype(jnp.bfloat16)
        for k in range(sources):
            out_refs[k][spans[g], :] = result[k * rows_doc : (k + 1) * rows_doc]


def assemble_kernel(n_head, steps, *refs):
    block_refs, out_ref, sems = refs[: len(steps)], refs[-2], refs[-1]
    me = lax.axis_index("head")
    width = block_refs[0].shape[1]
    copies = []
    for at, step in enumerate(steps):
        column = pl.multiple_of(peer_of_traced(me, step, n_head) * width, width)
        copies.append(
            pltpu.make_async_copy(block_refs[at], out_ref.at[:, pl.ds(column, width)], sems.at[at])
        )
    for copy in copies:
        copy.start()
    for copy in copies:
        copy.wait()


def peer_of_traced(index, step, count):
    if count & (count - 1) == 0:
        return index ^ step
    return lax.rem(index + step, count)


def shards(
    queries,
    doc_of,
    doc_lengths,
    rotated_key_levels,
    rotated_value_levels,
    key_level_scale,
    value_level_scale,
):
    rows_home, width = queries.shape
    heads_dev = width // HEAD_WIDTH
    kv_dev = key_level_scale.shape[1]
    shard_len = rotated_key_levels.shape[1]
    n_doc = lax.axis_size("doc")
    n_ctx = lax.axis_size("ctx")
    n_head = lax.axis_size("head")
    cap = max(2, 3 * rows_home // (2 * n_doc))
    params = pltpu.CompilerParams(vmem_limit_bytes=VMEM_BYTES)
    vmem = pl.BlockSpec(memory_space=pltpu.VMEM)
    slots = heads_dev * cap
    slot_block = jax.ShapeDtypeStruct((slots, HEAD_WIDTH), jnp.bfloat16)

    key_block, value_block = rotated_key_levels[0], rotated_value_levels[0]
    args = (
        doc_of.reshape(1, rows_home),
        doc_lengths.reshape(1, doc_lengths.shape[0]),
        queries,
        key_block,
        value_block,
        key_level_scale[0],
        value_level_scale[0],
    )
    placing_block = jax.ShapeDtypeStruct((n_doc * (LANES // rows_home) * cap, LANES), jnp.bfloat16)
    hbm = pl.BlockSpec(memory_space=pltpu.HBM)
    anywhere = pl.BlockSpec(memory_space=pl.ANY)
    cache_rows = 2 * shard_len + 2 * shard_len // HEAD_WIDTH
    placing, valid, own_cache, *outgoing = pl.pallas_call(
        functools.partial(dispatch_kernel, n_doc, n_ctx, cap),
        out_shape=[
            placing_block,
            jax.ShapeDtypeStruct((n_ctx, shard_len), jnp.float32),
            jax.ShapeDtypeStruct((cache_rows, kv_dev * HEAD_WIDTH), key_block.dtype),
        ]
        + [slot_block] * n_doc,
        in_specs=[hbm] * len(args),
        out_specs=[vmem] * (n_doc + 3),
        scratch_shapes=[
            pltpu.VMEM(args[at].shape, args[at].dtype) for at in (0, 1, 2, 5, 6)
        ]
        + [pltpu.SemaphoreType.DMA((len(args),))],
        compiler_params=params,
    )(*[pltpu.with_memory_space_constraint(arg, pltpu.HBM) for arg in args])
    cache = [own_cache]
    for step in range(1, n_ctx):
        cache.append(
            lax.ppermute(own_cache, "ctx", [(i, (i + step) % n_ctx) for i in range(n_ctx)])
        )
    arrived = [outgoing[0]] + [sent(outgoing[k], "doc", k) for k in range(1, n_doc)]

    def attended_for(steps, valid):
        sources = [arrived[k] for k in steps]
        rows = len(sources) * slots
        return pl.pallas_call(
            functools.partial(attend_kernel, len(sources), n_ctx, kv_dev),
            out_shape=[slot_block] * len(sources),
            in_specs=[vmem] * (1 + len(sources) + n_ctx),
            out_specs=[vmem] * len(sources),
            compiler_params=params,
            cost_estimate=pl.CostEstimate(
                flops=4 * rows * n_ctx * shard_len * HEAD_WIDTH,
                bytes_accessed=4 * n_ctx * shard_len * kv_dev * HEAD_WIDTH,
                transcendentals=rows * n_ctx * shard_len,
            ),
        )(valid, *sources, *cache)

    finished = {}
    for steps in (range(1, n_doc - 1), range(max(1, n_doc - 1), n_doc)):
        if len(steps) > 0:
            finished.update(zip(steps, attended_for(steps, valid)))
    if n_doc > 1:
        finished[n_doc - 1], valid = lax.optimization_barrier((finished[n_doc - 1], valid))
    finished[0] = attended_for((0,), valid)[0]
    back = [finished[0]] + [returned(finished[k], "doc", k) for k in range(1, n_doc)]

    mine = pl.pallas_call(
        functools.partial(collect_kernel, n_doc, cap),
        out_shape=jax.ShapeDtypeStruct((rows_home, width), jnp.bfloat16),
        in_specs=[vmem] * (1 + n_doc),
        out_specs=vmem,
        compiler_params=params,
    )(placing, *back)

    def assembled(steps, before):
        return pl.pallas_call(
            functools.partial(assemble_kernel, n_head, steps),
            out_shape=jax.ShapeDtypeStruct((rows_home, n_head * width), jnp.bfloat16),
            in_specs=[anywhere] * len(steps) + [hbm] * len(before),
            out_specs=hbm,
            scratch_shapes=[pltpu.SemaphoreType.DMA((len(steps),))],
            input_output_aliases={len(steps): 0} if before else {},
            compiler_params=params,
        )(*[blocks[step] for step in steps], *before)

    order = sorted(range(1, n_head), key=lambda step: (step % 2, step))
    blocks = {0: mine}
    for step in order:
        blocks[step] = returned(mine, "head", step)
    if len(order) < 2:
        return assembled([0] + order, ())
    attended = assembled([0, order[0]], ())
    return assembled(order[:0:-1], (attended,))


def solution(mesh):
    in_specs = (
        P(("doc", "ctx"), "head"),
        P(("doc", "ctx"), None),
        P(),
        P("doc", "ctx", "head"),
        P("doc", "ctx", "head"),
        P("doc", "head", "ctx"),
        P("doc", "head", "ctx"),
    )
    out_specs = P(("doc", "ctx"), None)
    return jax.shard_map(shards, mesh=mesh, in_specs=in_specs, out_specs=out_specs, check_vma=False)
```

```python
import functools
import math

import jax
import jax.numpy as jnp
from jax import lax
from jax.experimental import pallas as pl
from jax.experimental.pallas import tpu as pltpu
from jax.sharding import PartitionSpec as P

HEAD_WIDTH = 128
LANES = 128
VMEM_BYTES = 40 * 1024 * 1024


def peer_of(index, step, count):
    if count & (count - 1) == 0:
        return index ^ step
    return (index + step) % count


def sent(value, axis, step):
    count = lax.axis_size(axis)
    return lax.ppermute(value, axis, [(i, peer_of(i, step, count)) for i in range(count)])


def returned(value, axis, step):
    count = lax.axis_size(axis)
    return lax.ppermute(value, axis, [(peer_of(i, step, count), i) for i in range(count)])


def sign_matrix():
    row = lax.broadcasted_iota(jnp.int32, (HEAD_WIDTH, HEAD_WIDTH), 0)
    column = lax.broadcasted_iota(jnp.int32, (HEAD_WIDTH, HEAD_WIDTH), 1)
    both = row & column
    both = both ^ (both >> 4)
    both = both ^ (both >> 2)
    both = both ^ (both >> 1)
    return (1 - 2 * (both & 1)).astype(jnp.float32).astype(jnp.bfloat16)


def placing_matrix(doc_row, n_doc, cap):
    rows = doc_row.shape[1]
    group = LANES // rows
    me = lax.axis_index("doc")
    square = (rows, rows)
    diagonal = lax.broadcasted_iota(jnp.int32, square, 0) == lax.broadcasted_iota(
        jnp.int32, square, 1
    )
    doc_column = jnp.sum(
        jnp.where(diagonal, jnp.broadcast_to(doc_row, square), 0), axis=1, keepdims=True
    )
    request = lax.broadcasted_iota(jnp.int32, (rows, LANES), 0)
    lane = lax.broadcasted_iota(jnp.int32, (rows, LANES), 1)
    docs = jnp.broadcast_to(doc_column, (rows, LANES))
    lane_request = lane % rows
    lane_doc = jnp.sum(jnp.where(request == lane_request, docs, 0), axis=0, keepdims=True)
    rank = jnp.sum(
        jnp.where((docs == lane_doc) & (request < lane_request), 1, 0), axis=0, keepdims=True
    )
    if n_doc & (n_doc - 1) == 0:
        step = lane_doc ^ me
    else:
        step = (lane_doc - me + n_doc) % n_doc
    place = step * (group * cap) + (lane[:1] // rows) * cap + rank
    slots = n_doc * group * cap
    slot = lax.broadcasted_iota(jnp.int32, (slots, LANES), 0)
    return jnp.where(slot == place, 1.0, 0.0).astype(jnp.bfloat16)


def dispatch_kernel(
    n_doc,
    n_ctx,
    cap,
    doc_hbm,
    length_hbm,
    query_hbm,
    key_hbm,
    value_hbm,
    key_scale_hbm,
    value_scale_hbm,
    placing_ref,
    valid_ref,
    cache_ref,
    *refs,
):
    out_refs, (doc_ref, length_ref, query_ref, key_scale_ref, value_scale_ref, sems) = (
        refs[:n_doc],
        refs[n_doc:],
    )
    shard_len, span = key_hbm.shape
    pairs = (
        (doc_hbm, doc_ref),
        (query_hbm, query_ref),
        (length_hbm, length_ref),
        (key_scale_hbm, key_scale_ref),
        (value_scale_hbm, value_scale_ref),
        (key_hbm, cache_ref.at[pl.ds(0, shard_len)]),
        (value_hbm, cache_ref.at[pl.ds(shard_len, shard_len)]),
    )
    copies = [
        pltpu.make_async_copy(source, target, sems.at[at])
        for at, (source, target) in enumerate(pairs)
    ]
    for copy in copies:
        copy.start()
    rows, width = query_ref.shape
    group = LANES // rows
    heads = width // HEAD_WIDTH
    block = group * cap
    signs = sign_matrix()
    scale = 1.0 / math.sqrt(HEAD_WIDTH)
    copies[0].wait()
    placing = placing_matrix(doc_ref[...], n_doc, cap)
    placing_ref[...] = placing
    copies[1].wait()
    rotated = []
    for g in range(heads // group):
        stacked = jnp.concatenate(
            [
                query_ref[:, (g * group + h) * HEAD_WIDTH : (g * group + h + 1) * HEAD_WIDTH]
                for h in range(group)
            ],
            axis=0,
        )
        product = jnp.dot(stacked, signs, preferred_element_type=jnp.float32) * scale
        rotated.append(product.astype(jnp.bfloat16))
    for g in range(heads // group):
        placed = jnp.dot(placing, rotated[g], preferred_element_type=jnp.float32).astype(
            jnp.bfloat16
        )
        for k in range(n_doc):
            out_refs[k][g * block : (g + 1) * block, :] = placed[k * block : (k + 1) * block]
    for copy in copies[2:5]:
        copy.wait()
    scale_rows = []
    for scale_ref in (key_scale_ref, value_scale_ref):
        scales = scale_ref[...].astype(jnp.float32)
        scale_rows += [
            scales[row : row + 1, at : at + span]
            for row in range(scales.shape[0])
            for at in range(0, shard_len, span)
        ]
    cache_ref[2 * shard_len :, :] = jnp.concatenate(scale_rows, axis=0).astype(jnp.bfloat16)
    lengths = length_ref[...]
    lane = lax.broadcasted_iota(jnp.int32, lengths.shape, 1)
    length = jnp.sum(
        jnp.where(lane == lax.axis_index("doc"), lengths, 0), axis=1, keepdims=True
    )
    step = lax.broadcasted_iota(jnp.int32, valid_ref.shape, 0)
    anchor = (lax.axis_index("ctx") - step + n_ctx) % n_ctx
    position = lax.broadcasted_iota(jnp.int32, valid_ref.shape, 1) + anchor * shard_len
    valid_ref[...] = jnp.where(position < length, 1.0, 0.0)
    for copy in copies[5:]:
        copy.wait()


def collect_kernel(n_doc, cap, placing_ref, *refs):
    back_refs, out_ref = refs[:n_doc], refs[n_doc]
    rows, width = out_ref.shape
    group = LANES // rows
    heads = width // HEAD_WIDTH
    block = group * cap
    placing = placing_ref[...]
    for g in range(heads // group):
        slots = jnp.concatenate(
            [back_refs[k][g * block : (g + 1) * block, :] for k in range(n_doc)], axis=0
        )
        mine = lax.dot_general(
            placing, slots, (((0,), (0,)), ((), ())), preferred_element_type=jnp.float32
        ).astype(jnp.bfloat16)
        for h in range(group):
            at = (g * group + h) * HEAD_WIDTH
            out_ref[:, at : at + HEAD_WIDTH] = mine[h * rows : (h + 1) * rows]


def attend_kernel(sources, n_ctx, kv_dev, valid_ref, *refs):
    query_refs, refs = refs[:sources], refs[sources:]
    cache_refs, out_refs = refs[:n_ctx], refs[n_ctx:]
    shard_len = valid_ref.shape[1]
    span = kv_dev * HEAD_WIDTH
    pieces = shard_len // span

    def scale_row(scales, row):
        return jnp.concatenate(
            [scales[row * pieces + at : row * pieces + at + 1, :] for at in range(pieces)], axis=1
        )

    rows_doc = query_refs[0].shape[0] // kv_dev
    signs = sign_matrix()
    scale = 1.0 / math.sqrt(HEAD_WIDTH)
    groups = range(kv_dev)
    spans = [slice(g * rows_doc, (g + 1) * rows_doc) for g in groups]
    heads = [slice(g * HEAD_WIDTH, (g + 1) * HEAD_WIDTH) for g in groups]
    rows = [jnp.concatenate([ref[span, :] for ref in query_refs], axis=0) for span in spans]
    states = [None] * kv_dev
    for first in range(0, n_ctx, 2):
        steps = range(first, min(first + 2, n_ctx))
        scales = {step: cache_refs[step][2 * shard_len :, :].astype(jnp.float32) for step in steps}
        valid = {step: valid_ref[step : step + 1, :] > 0.0 for step in steps}
        scores = {}
        for g in groups:
            for step in steps:
                key_scale = scale_row(scales[step], g) * (scale * math.log2(math.e))
                product = lax.dot_general(
                    rows[g],
                    cache_refs[step][:shard_len, heads[g]],
                    (((1,), (1,)), ((), ())),
                    preferred_element_type=jnp.float32,
                )
                scores[g, step] = jnp.where(valid[step], product * key_scale, -1e30)
        tops = []
        for g in groups:
            top = functools.reduce(
                jnp.maximum, [jnp.max(scores[g, step], axis=-1, keepdims=True) for step in steps]
            )
            tops.append(top if states[g] is None else jnp.maximum(top, states[g][0]))
        for g in groups:
            all_probs, summed = 0.0, 0.0
            for step in steps:
                value_scale = scale_row(scales[step], kv_dev + g)
                probs = jnp.exp2(scores[g, step] - tops[g])
                all_probs = all_probs + probs
                weights = (probs * value_scale).astype(jnp.bfloat16)
                summed = summed + jnp.dot(
                    weights,
                    cache_refs[step][shard_len : 2 * shard_len, heads[g]],
                    preferred_element_type=jnp.float32,
                )
            total = jnp.sum(all_probs, axis=-1, keepdims=True)
            if states[g] is not None:
                factor = jnp.exp2(states[g][0] - tops[g])
                total = total + states[g][1] * factor
                summed = summed + states[g][2] * factor
            states[g] = (tops[g], total, summed)
    for g in groups:
        _, total, summed = states[g]
        mixed = summed * (scale / total)
        high = mixed.astype(jnp.bfloat16)
        low = (mixed - high.astype(jnp.float32)).astype(jnp.bfloat16)
        result = jnp.dot(high, signs, preferred_element_type=jnp.float32) + jnp.dot(
            low, signs, preferred_element_type=jnp.float32
        )
        result = result.astype(jnp.bfloat16)
        for k in range(sources):
            out_refs[k][spans[g], :] = result[k * rows_doc : (k + 1) * rows_doc]


def assemble_kernel(n_head, steps, *refs):
    block_refs, out_ref, sems = refs[: len(steps)], refs[-2], refs[-1]
    me = lax.axis_index("head")
    width = block_refs[0].shape[1]
    copies = []
    for at, step in enumerate(steps):
        column = pl.multiple_of(peer_of_traced(me, step, n_head) * width, width)
        copies.append(
            pltpu.make_async_copy(block_refs[at], out_ref.at[:, pl.ds(column, width)], sems.at[at])
        )
    for copy in copies:
        copy.start()
    for copy in copies:
        copy.wait()


def peer_of_traced(index, step, count):
    if count & (count - 1) == 0:
        return index ^ step
    return lax.rem(index + step, count)


def shards(
    queries,
    doc_of,
    doc_lengths,
    rotated_key_levels,
    rotated_value_levels,
    key_level_scale,
    value_level_scale,
):
    rows_home, width = queries.shape
    heads_dev = width // HEAD_WIDTH
    kv_dev = key_level_scale.shape[1]
    shard_len = rotated_key_levels.shape[1]
    n_doc = lax.axis_size("doc")
    n_ctx = lax.axis_size("ctx")
    n_head = lax.axis_size("head")
    cap = max(2, 3 * rows_home // (2 * n_doc))
    params = pltpu.CompilerParams(vmem_limit_bytes=VMEM_BYTES)
    vmem = pl.BlockSpec(memory_space=pltpu.VMEM)
    slots = heads_dev * cap
    slot_block = jax.ShapeDtypeStruct((slots, HEAD_WIDTH), jnp.bfloat16)

    key_block, value_block = rotated_key_levels[0], rotated_value_levels[0]
    args = (
        doc_of.reshape(1, rows_home),
        doc_lengths.reshape(1, doc_lengths.shape[0]),
        queries,
        key_block,
        value_block,
        key_level_scale[0],
        value_level_scale[0],
    )
    placing_block = jax.ShapeDtypeStruct((n_doc * (LANES // rows_home) * cap, LANES), jnp.bfloat16)
    hbm = pl.BlockSpec(memory_space=pltpu.HBM)
    anywhere = pl.BlockSpec(memory_space=pl.ANY)
    cache_rows = 2 * shard_len + 2 * shard_len // HEAD_WIDTH
    placing, valid, own_cache, *outgoing = pl.pallas_call(
        functools.partial(dispatch_kernel, n_doc, n_ctx, cap),
        out_shape=[
            placing_block,
            jax.ShapeDtypeStruct((n_ctx, shard_len), jnp.float32),
            jax.ShapeDtypeStruct((cache_rows, kv_dev * HEAD_WIDTH), key_block.dtype),
        ]
        + [slot_block] * n_doc,
        in_specs=[hbm] * len(args),
        out_specs=[vmem] * (n_doc + 3),
        scratch_shapes=[
            pltpu.VMEM(args[at].shape, args[at].dtype) for at in (0, 1, 2, 5, 6)
        ]
        + [pltpu.SemaphoreType.DMA((len(args),))],
        compiler_params=params,
    )(*[pltpu.with_memory_space_constraint(arg, pltpu.HBM) for arg in args])
    cache = [own_cache]
    for step in range(1, n_ctx):
        cache.append(
            lax.ppermute(own_cache, "ctx", [(i, (i + step) % n_ctx) for i in range(n_ctx)])
        )
    arrived = [outgoing[0]] + [sent(outgoing[k], "doc", k) for k in range(1, n_doc)]

    def attended_for(steps, valid):
        sources = [arrived[k] for k in steps]
        rows = len(sources) * slots
        return pl.pallas_call(
            functools.partial(attend_kernel, len(sources), n_ctx, kv_dev),
            out_shape=[slot_block] * len(sources),
            in_specs=[vmem] * (1 + len(sources) + n_ctx),
            out_specs=[vmem] * len(sources),
            compiler_params=params,
            cost_estimate=pl.CostEstimate(
                flops=4 * rows * n_ctx * shard_len * HEAD_WIDTH,
                bytes_accessed=4 * n_ctx * shard_len * kv_dev * HEAD_WIDTH,
                transcendentals=rows * n_ctx * shard_len,
            ),
        )(valid, *sources, *cache)

    finished = {}
    for steps in (range(1, n_doc - 1), range(max(1, n_doc - 1), n_doc)):
        if len(steps) > 0:
            finished.update(zip(steps, attended_for(steps, valid)))
    if n_doc > 1:
        finished[n_doc - 1], valid = lax.optimization_barrier((finished[n_doc - 1], valid))
    finished[0] = attended_for((0,), valid)[0]
    back = [finished[0]] + [returned(finished[k], "doc", k) for k in range(1, n_doc)]

    mine = pl.pallas_call(
        functools.partial(collect_kernel, n_doc, cap),
        out_shape=jax.ShapeDtypeStruct((rows_home, width), jnp.bfloat16),
        in_specs=[vmem] * (1 + n_doc),
        out_specs=vmem,
        compiler_params=params,
    )(placing, *back)

    def assembled(steps, before):
        return pl.pallas_call(
            functools.partial(assemble_kernel, n_head, steps),
            out_shape=jax.ShapeDtypeStruct((rows_home, n_head * width), jnp.bfloat16),
            in_specs=[anywhere] * len(steps) + [hbm] * len(before),
            out_specs=hbm,
            scratch_shapes=[pltpu.SemaphoreType.DMA((len(steps),))],
            input_output_aliases={len(steps): 0} if before else {},
            compiler_params=params,
        )(*[blocks[step] for step in steps], *before)

    order = sorted(range(1, n_head), key=lambda step: (step % 2, step))
    blocks = {0: mine}
    for step in order:
        blocks[step] = returned(mine, "head", step)
    if len(order) < 2:
        return assembled([0] + order, ())
    attended = assembled([0, order[0]], ())
    for step in order[1:]:
        attended = assembled([step], (attended,))
    return attended


def solution(mesh):
    in_specs = (
        P(("doc", "ctx"), "head"),
        P(("doc", "ctx"), None),
        P(),
        P("doc", "ctx", "head"),
        P("doc", "ctx", "head"),
        P("doc", "head", "ctx"),
        P("doc", "head", "ctx"),
    )
    out_specs = P(("doc", "ctx"), None)
    return jax.shard_map(shards, mesh=mesh, in_specs=in_specs, out_specs=out_specs, check_vma=False)
```

```python
import functools
import math

import jax
import jax.numpy as jnp
from jax import lax
from jax.experimental import pallas as pl
from jax.experimental.pallas import tpu as pltpu
from jax.sharding import PartitionSpec as P

HEAD_WIDTH = 128
LANES = 128
VMEM_BYTES = 40 * 1024 * 1024


def peer_of(index, step, count):
    if count & (count - 1) == 0:
        return index ^ step
    return (index + step) % count


def sent(value, axis, step):
    count = lax.axis_size(axis)
    return lax.ppermute(value, axis, [(i, peer_of(i, step, count)) for i in range(count)])


def returned(value, axis, step):
    count = lax.axis_size(axis)
    return lax.ppermute(value, axis, [(peer_of(i, step, count), i) for i in range(count)])


def sign_matrix():
    row = lax.broadcasted_iota(jnp.int32, (HEAD_WIDTH, HEAD_WIDTH), 0)
    column = lax.broadcasted_iota(jnp.int32, (HEAD_WIDTH, HEAD_WIDTH), 1)
    both = row & column
    both = both ^ (both >> 4)
    both = both ^ (both >> 2)
    both = both ^ (both >> 1)
    return (1 - 2 * (both & 1)).astype(jnp.float32).astype(jnp.bfloat16)


def placing_matrix(doc_row, n_doc, cap):
    rows = doc_row.shape[1]
    group = LANES // rows
    me = lax.axis_index("doc")
    square = (rows, rows)
    diagonal = lax.broadcasted_iota(jnp.int32, square, 0) == lax.broadcasted_iota(
        jnp.int32, square, 1
    )
    doc_column = jnp.sum(
        jnp.where(diagonal, jnp.broadcast_to(doc_row, square), 0), axis=1, keepdims=True
    )
    request = lax.broadcasted_iota(jnp.int32, (rows, LANES), 0)
    lane = lax.broadcasted_iota(jnp.int32, (rows, LANES), 1)
    docs = jnp.broadcast_to(doc_column, (rows, LANES))
    lane_request = lane % rows
    lane_doc = jnp.sum(jnp.where(request == lane_request, docs, 0), axis=0, keepdims=True)
    rank = jnp.sum(
        jnp.where((docs == lane_doc) & (request < lane_request), 1, 0), axis=0, keepdims=True
    )
    if n_doc & (n_doc - 1) == 0:
        step = lane_doc ^ me
    else:
        step = (lane_doc - me + n_doc) % n_doc
    place = step * (group * cap) + (lane[:1] // rows) * cap + rank
    slots = n_doc * group * cap
    slot = lax.broadcasted_iota(jnp.int32, (slots, LANES), 0)
    return jnp.where(slot == place, 1.0, 0.0).astype(jnp.bfloat16)


def dispatch_kernel(
    n_doc,
    n_ctx,
    cap,
    doc_hbm,
    length_hbm,
    query_hbm,
    key_hbm,
    value_hbm,
    key_scale_hbm,
    value_scale_hbm,
    placing_ref,
    valid_ref,
    cache_ref,
    *refs,
):
    out_refs, (doc_ref, length_ref, query_ref, key_scale_ref, value_scale_ref, sems) = (
        refs[:n_doc],
        refs[n_doc:],
    )
    shard_len, span = key_hbm.shape
    pairs = (
        (doc_hbm, doc_ref),
        (query_hbm, query_ref),
        (length_hbm, length_ref),
        (key_scale_hbm, key_scale_ref),
        (value_scale_hbm, value_scale_ref),
        (key_hbm, cache_ref.at[pl.ds(0, shard_len)]),
        (value_hbm, cache_ref.at[pl.ds(shard_len, shard_len)]),
    )
    copies = [
        pltpu.make_async_copy(source, target, sems.at[at])
        for at, (source, target) in enumerate(pairs)
    ]
    for copy in copies:
        copy.start()
    rows, width = query_ref.shape
    group = LANES // rows
    heads = width // HEAD_WIDTH
    block = group * cap
    signs = sign_matrix()
    scale = 1.0 / math.sqrt(HEAD_WIDTH)
    copies[0].wait()
    placing = placing_matrix(doc_ref[...], n_doc, cap)
    placing_ref[...] = placing
    copies[1].wait()
    rotated = []
    for g in range(heads // group):
        stacked = jnp.concatenate(
            [
                query_ref[:, (g * group + h) * HEAD_WIDTH : (g * group + h + 1) * HEAD_WIDTH]
                for h in range(group)
            ],
            axis=0,
        )
        product = jnp.dot(stacked, signs, preferred_element_type=jnp.float32) * scale
        rotated.append(product.astype(jnp.bfloat16))
    for g in range(heads // group):
        placed = jnp.dot(placing, rotated[g], preferred_element_type=jnp.float32).astype(
            jnp.bfloat16
        )
        for k in range(n_doc):
            out_refs[k][g * block : (g + 1) * block, :] = placed[k * block : (k + 1) * block]
    for copy in copies[2:5]:
        copy.wait()
    scale_rows = []
    for scale_ref in (key_scale_ref, value_scale_ref):
        scales = scale_ref[...].astype(jnp.float32)
        scale_rows += [
            scales[row : row + 1, at : at + span]
            for row in range(scales.shape[0])
            for at in range(0, shard_len, span)
        ]
    cache_ref[2 * shard_len :, :] = jnp.concatenate(scale_rows, axis=0).astype(jnp.bfloat16)
    lengths = length_ref[...]
    lane = lax.broadcasted_iota(jnp.int32, lengths.shape, 1)
    length = jnp.sum(
        jnp.where(lane == lax.axis_index("doc"), lengths, 0), axis=1, keepdims=True
    )
    step = lax.broadcasted_iota(jnp.int32, valid_ref.shape, 0)
    anchor = (lax.axis_index("ctx") - step + n_ctx) % n_ctx
    position = lax.broadcasted_iota(jnp.int32, valid_ref.shape, 1) + anchor * shard_len
    valid_ref[...] = jnp.where(position < length, 1.0, 0.0)
    for copy in copies[5:]:
        copy.wait()


def turn_kernel(placing_ref, after_ref, out_ref):
    out_ref[...] = placing_ref[...].astype(jnp.float32).T.astype(jnp.bfloat16)


def collect_kernel(n_doc, cap, placing_ref, *refs):
    back_refs, out_ref = refs[:n_doc], refs[n_doc]
    rows, width = out_ref.shape
    group = LANES // rows
    heads = width // HEAD_WIDTH
    block = group * cap
    placing = placing_ref[...]
    for g in range(heads // group):
        slots = jnp.concatenate(
            [back_refs[k][g * block : (g + 1) * block, :] for k in range(n_doc)], axis=0
        )
        mine = jnp.dot(placing, slots, preferred_element_type=jnp.float32).astype(jnp.bfloat16)
        for h in range(group):
            at = (g * group + h) * HEAD_WIDTH
            out_ref[:, at : at + HEAD_WIDTH] = mine[h * rows : (h + 1) * rows]


def attend_kernel(sources, n_ctx, kv_dev, valid_ref, *refs):
    query_refs, refs = refs[:sources], refs[sources:]
    cache_refs, out_refs = refs[:n_ctx], refs[n_ctx:]
    shard_len = valid_ref.shape[1]
    span = kv_dev * HEAD_WIDTH
    pieces = shard_len // span

    def scale_row(scales, row):
        return jnp.concatenate(
            [scales[row * pieces + at : row * pieces + at + 1, :] for at in range(pieces)], axis=1
        )

    rows_doc = query_refs[0].shape[0] // kv_dev
    signs = sign_matrix()
    scale = 1.0 / math.sqrt(HEAD_WIDTH)
    groups = range(kv_dev)
    spans = [slice(g * rows_doc, (g + 1) * rows_doc) for g in groups]
    heads = [slice(g * HEAD_WIDTH, (g + 1) * HEAD_WIDTH) for g in groups]
    rows = [jnp.concatenate([ref[span, :] for ref in query_refs], axis=0) for span in spans]
    states = [None] * kv_dev
    for first in range(0, n_ctx, 2):
        steps = range(first, min(first + 2, n_ctx))
        scales = {step: cache_refs[step][2 * shard_len :, :].astype(jnp.float32) for step in steps}
        valid = {step: valid_ref[step : step + 1, :] > 0.0 for step in steps}
        scores = {}
        for g in groups:
            for step in steps:
                key_scale = scale_row(scales[step], g) * (scale * math.log2(math.e))
                product = lax.dot_general(
                    rows[g],
                    cache_refs[step][:shard_len, heads[g]],
                    (((1,), (1,)), ((), ())),
                    preferred_element_type=jnp.float32,
                )
                scores[g, step] = jnp.where(valid[step], product * key_scale, -1e30)
        tops = []
        for g in groups:
            top = functools.reduce(
                jnp.maximum, [jnp.max(scores[g, step], axis=-1, keepdims=True) for step in steps]
            )
            tops.append(top if states[g] is None else jnp.maximum(top, states[g][0]))
        for g in groups:
            all_probs, summed = 0.0, 0.0
            for step in steps:
                value_scale = scale_row(scales[step], kv_dev + g)
                probs = jnp.exp2(scores[g, step] - tops[g])
                all_probs = all_probs + probs
                weights = (probs * value_scale).astype(jnp.bfloat16)
                summed = summed + jnp.dot(
                    weights,
                    cache_refs[step][shard_len : 2 * shard_len, heads[g]],
                    preferred_element_type=jnp.float32,
                )
            total = jnp.sum(all_probs, axis=-1, keepdims=True)
            if states[g] is not None:
                factor = jnp.exp2(states[g][0] - tops[g])
                total = total + states[g][1] * factor
                summed = summed + states[g][2] * factor
            states[g] = (tops[g], total, summed)
    for g in groups:
        _, total, summed = states[g]
        mixed = summed * (scale / total)
        high = mixed.astype(jnp.bfloat16)
        low = (mixed - high.astype(jnp.float32)).astype(jnp.bfloat16)
        result = jnp.dot(high, signs, preferred_element_type=jnp.float32) + jnp.dot(
            low, signs, preferred_element_type=jnp.float32
        )
        result = result.astype(jnp.bfloat16)
        for k in range(sources):
            out_refs[k][spans[g], :] = result[k * rows_doc : (k + 1) * rows_doc]


def assemble_kernel(n_head, steps, *refs):
    block_refs, out_ref, sems = refs[: len(steps)], refs[-2], refs[-1]
    me = lax.axis_index("head")
    width = block_refs[0].shape[1]
    copies = []
    for at, step in enumerate(steps):
        column = pl.multiple_of(peer_of_traced(me, step, n_head) * width, width)
        copies.append(
            pltpu.make_async_copy(block_refs[at], out_ref.at[:, pl.ds(column, width)], sems.at[at])
        )
    for copy in copies:
        copy.start()
    for copy in copies:
        copy.wait()


def peer_of_traced(index, step, count):
    if count & (count - 1) == 0:
        return index ^ step
    return lax.rem(index + step, count)


def shards(
    queries,
    doc_of,
    doc_lengths,
    rotated_key_levels,
    rotated_value_levels,
    key_level_scale,
    value_level_scale,
):
    rows_home, width = queries.shape
    heads_dev = width // HEAD_WIDTH
    kv_dev = key_level_scale.shape[1]
    shard_len = rotated_key_levels.shape[1]
    n_doc = lax.axis_size("doc")
    n_ctx = lax.axis_size("ctx")
    n_head = lax.axis_size("head")
    cap = max(2, 3 * rows_home // (2 * n_doc))
    params = pltpu.CompilerParams(vmem_limit_bytes=VMEM_BYTES)
    vmem = pl.BlockSpec(memory_space=pltpu.VMEM)
    slots = heads_dev * cap
    slot_block = jax.ShapeDtypeStruct((slots, HEAD_WIDTH), jnp.bfloat16)

    key_block, value_block = rotated_key_levels[0], rotated_value_levels[0]
    args = (
        doc_of.reshape(1, rows_home),
        doc_lengths.reshape(1, doc_lengths.shape[0]),
        queries,
        key_block,
        value_block,
        key_level_scale[0],
        value_level_scale[0],
    )
    placing_block = jax.ShapeDtypeStruct((n_doc * (LANES // rows_home) * cap, LANES), jnp.bfloat16)
    hbm = pl.BlockSpec(memory_space=pltpu.HBM)
    anywhere = pl.BlockSpec(memory_space=pl.ANY)
    cache_rows = 2 * shard_len + 2 * shard_len // HEAD_WIDTH
    placing, valid, own_cache, *outgoing = pl.pallas_call(
        functools.partial(dispatch_kernel, n_doc, n_ctx, cap),
        out_shape=[
            placing_block,
            jax.ShapeDtypeStruct((n_ctx, shard_len), jnp.float32),
            jax.ShapeDtypeStruct((cache_rows, kv_dev * HEAD_WIDTH), key_block.dtype),
        ]
        + [slot_block] * n_doc,
        in_specs=[hbm] * len(args),
        out_specs=[vmem] * (n_doc + 3),
        scratch_shapes=[
            pltpu.VMEM(args[at].shape, args[at].dtype) for at in (0, 1, 2, 5, 6)
        ]
        + [pltpu.SemaphoreType.DMA((len(args),))],
        compiler_params=params,
    )(*[pltpu.with_memory_space_constraint(arg, pltpu.HBM) for arg in args])
    cache = [own_cache]
    for step in range(1, n_ctx):
        cache.append(
            lax.ppermute(own_cache, "ctx", [(i, (i + step) % n_ctx) for i in range(n_ctx)])
        )
    arrived = [outgoing[0]] + [sent(outgoing[k], "doc", k) for k in range(1, n_doc)]

    def attended_for(steps, valid):
        sources = [arrived[k] for k in steps]
        rows = len(sources) * slots
        return pl.pallas_call(
            functools.partial(attend_kernel, len(sources), n_ctx, kv_dev),
            out_shape=[slot_block] * len(sources),
            in_specs=[vmem] * (1 + len(sources) + n_ctx),
            out_specs=[vmem] * len(sources),
            compiler_params=params,
            cost_estimate=pl.CostEstimate(
                flops=4 * rows * n_ctx * shard_len * HEAD_WIDTH,
                bytes_accessed=4 * n_ctx * shard_len * kv_dev * HEAD_WIDTH,
                transcendentals=rows * n_ctx * shard_len,
            ),
        )(valid, *sources, *cache)

    finished = {}
    for steps in (range(1, n_doc - 1), range(max(1, n_doc - 1), n_doc)):
        if len(steps) > 0:
            finished.update(zip(steps, attended_for(steps, valid)))
    if n_doc > 1:
        finished[n_doc - 1], valid = lax.optimization_barrier((finished[n_doc - 1], valid))
    finished[0] = attended_for((0,), valid)[0]
    back = [finished[0]] + [returned(finished[k], "doc", k) for k in range(1, n_doc)]

    turned = pl.pallas_call(
        turn_kernel,
        out_shape=jax.ShapeDtypeStruct(placing.shape[::-1], placing.dtype),
        in_specs=[vmem, anywhere],
        out_specs=vmem,
        compiler_params=params,
    )(placing, finished[0])
    mine = pl.pallas_call(
        functools.partial(collect_kernel, n_doc, cap),
        out_shape=jax.ShapeDtypeStruct((rows_home, width), jnp.bfloat16),
        in_specs=[vmem] * (1 + n_doc),
        out_specs=vmem,
        compiler_params=params,
    )(turned, *back)

    def assembled(steps, before):
        return pl.pallas_call(
            functools.partial(assemble_kernel, n_head, steps),
            out_shape=jax.ShapeDtypeStruct((rows_home, n_head * width), jnp.bfloat16),
            in_specs=[anywhere] * len(steps) + [hbm] * len(before),
            out_specs=hbm,
            scratch_shapes=[pltpu.SemaphoreType.DMA((len(steps),))],
            input_output_aliases={len(steps): 0} if before else {},
            compiler_params=params,
        )(*[blocks[step] for step in steps], *before)

    order = sorted(range(1, n_head), key=lambda step: (step % 2, step))
    blocks = {0: mine}
    for step in order:
        blocks[step] = returned(mine, "head", step)
    if len(order) < 2:
        return assembled([0] + order, ())
    attended = assembled([0, order[0]], ())
    for step in order[1:]:
        attended = assembled([step], (attended,))
    return attended


def solution(mesh):
    in_specs = (
        P(("doc", "ctx"), "head"),
        P(("doc", "ctx"), None),
        P(),
        P("doc", "ctx", "head"),
        P("doc", "ctx", "head"),
        P("doc", "head", "ctx"),
        P("doc", "head", "ctx"),
    )
    out_specs = P(("doc", "ctx"), None)
    return jax.shard_map(shards, mesh=mesh, in_specs=in_specs, out_specs=out_specs, check_vma=False)
```

```python
import functools
import math

import jax
import jax.numpy as jnp
from jax import lax
from jax.experimental import pallas as pl
from jax.experimental.pallas import tpu as pltpu
from jax.sharding import PartitionSpec as P

HEAD_WIDTH = 128
LANES = 128
VMEM_BYTES = 40 * 1024 * 1024


def peer_of(index, step, count):
    if count & (count - 1) == 0:
        return index ^ step
    return (index + step) % count


def sent(value, axis, step):
    count = lax.axis_size(axis)
    return lax.ppermute(value, axis, [(i, peer_of(i, step, count)) for i in range(count)])


def returned(value, axis, step):
    count = lax.axis_size(axis)
    return lax.ppermute(value, axis, [(peer_of(i, step, count), i) for i in range(count)])


def sign_matrix():
    row = lax.broadcasted_iota(jnp.int32, (HEAD_WIDTH, HEAD_WIDTH), 0)
    column = lax.broadcasted_iota(jnp.int32, (HEAD_WIDTH, HEAD_WIDTH), 1)
    both = row & column
    both = both ^ (both >> 4)
    both = both ^ (both >> 2)
    both = both ^ (both >> 1)
    return (1 - 2 * (both & 1)).astype(jnp.float32).astype(jnp.bfloat16)


def placing_matrix(doc_row, n_doc, cap):
    rows = doc_row.shape[1]
    group = LANES // rows
    me = lax.axis_index("doc")
    square = (rows, rows)
    diagonal = lax.broadcasted_iota(jnp.int32, square, 0) == lax.broadcasted_iota(
        jnp.int32, square, 1
    )
    doc_column = jnp.sum(
        jnp.where(diagonal, jnp.broadcast_to(doc_row, square), 0), axis=1, keepdims=True
    )
    request = lax.broadcasted_iota(jnp.int32, (rows, LANES), 0)
    lane = lax.broadcasted_iota(jnp.int32, (rows, LANES), 1)
    docs = jnp.broadcast_to(doc_column, (rows, LANES))
    lane_request = lane % rows
    lane_doc = jnp.sum(jnp.where(request == lane_request, docs, 0), axis=0, keepdims=True)
    rank = jnp.sum(
        jnp.where((docs == lane_doc) & (request < lane_request), 1, 0), axis=0, keepdims=True
    )
    if n_doc & (n_doc - 1) == 0:
        step = lane_doc ^ me
    else:
        step = (lane_doc - me + n_doc) % n_doc
    place = step * (group * cap) + (lane[:1] // rows) * cap + rank
    slots = n_doc * group * cap
    slot = lax.broadcasted_iota(jnp.int32, (slots, LANES), 0)
    return jnp.where(slot == place, 1.0, 0.0).astype(jnp.bfloat16)


def dispatch_kernel(
    n_doc,
    n_ctx,
    cap,
    doc_hbm,
    length_hbm,
    query_hbm,
    key_hbm,
    value_hbm,
    key_scale_hbm,
    value_scale_hbm,
    placing_ref,
    valid_ref,
    cache_ref,
    *refs,
):
    out_refs, (doc_ref, length_ref, query_ref, key_scale_ref, value_scale_ref, sems) = (
        refs[:n_doc],
        refs[n_doc:],
    )
    shard_len, span = key_hbm.shape
    pairs = (
        (doc_hbm, doc_ref),
        (query_hbm, query_ref),
        (length_hbm, length_ref),
        (key_scale_hbm, key_scale_ref),
        (value_scale_hbm, value_scale_ref),
        (key_hbm, cache_ref.at[pl.ds(0, shard_len)]),
        (value_hbm, cache_ref.at[pl.ds(shard_len, shard_len)]),
    )
    copies = [
        pltpu.make_async_copy(source, target, sems.at[at])
        for at, (source, target) in enumerate(pairs)
    ]
    for copy in copies:
        copy.start()
    rows, width = query_ref.shape
    group = LANES // rows
    heads = width // HEAD_WIDTH
    block = group * cap
    signs = sign_matrix()
    scale = 1.0 / math.sqrt(HEAD_WIDTH)
    copies[0].wait()
    placing = placing_matrix(doc_ref[...], n_doc, cap)
    placing_ref[...] = placing
    copies[1].wait()
    rotated = []
    for g in range(heads // group):
        stacked = jnp.concatenate(
            [
                query_ref[:, (g * group + h) * HEAD_WIDTH : (g * group + h + 1) * HEAD_WIDTH]
                for h in range(group)
            ],
            axis=0,
        )
        product = jnp.dot(stacked, signs, preferred_element_type=jnp.float32) * scale
        rotated.append(product.astype(jnp.bfloat16))
    for g in range(heads // group):
        placed = jnp.dot(placing, rotated[g], preferred_element_type=jnp.float32).astype(
            jnp.bfloat16
        )
        for k in range(n_doc):
            out_refs[k][g * block : (g + 1) * block, :] = placed[k * block : (k + 1) * block]
    for copy in copies[2:5]:
        copy.wait()
    scale_rows = []
    for scale_ref in (key_scale_ref, value_scale_ref):
        scales = scale_ref[...].astype(jnp.float32)
        scale_rows += [
            scales[row : row + 1, at : at + span]
            for row in range(scales.shape[0])
            for at in range(0, shard_len, span)
        ]
    cache_ref[2 * shard_len :, :] = jnp.concatenate(scale_rows, axis=0).astype(jnp.bfloat16)
    lengths = length_ref[...]
    lane = lax.broadcasted_iota(jnp.int32, lengths.shape, 1)
    length = jnp.sum(
        jnp.where(lane == lax.axis_index("doc"), lengths, 0), axis=1, keepdims=True
    )
    step = lax.broadcasted_iota(jnp.int32, valid_ref.shape, 0)
    anchor = (lax.axis_index("ctx") - step + n_ctx) % n_ctx
    position = lax.broadcasted_iota(jnp.int32, valid_ref.shape, 1) + anchor * shard_len
    valid_ref[...] = jnp.where(position < length, 1.0, 0.0)
    for copy in copies[5:]:
        copy.wait()


def turn_kernel(placing_ref, after_ref, out_ref):
    out_ref[...] = placing_ref[...].astype(jnp.float32).T.astype(jnp.bfloat16)


def collect_kernel(n_doc, cap, placing_ref, *refs):
    back_refs, out_ref = refs[:n_doc], refs[n_doc]
    rows, width = out_ref.shape
    group = LANES // rows
    heads = width // HEAD_WIDTH
    block = group * cap
    placing = placing_ref[...]
    for g in range(heads // group):
        slots = jnp.concatenate(
            [back_refs[k][g * block : (g + 1) * block, :] for k in range(n_doc)], axis=0
        )
        mine = jnp.dot(placing, slots, preferred_element_type=jnp.float32).astype(jnp.bfloat16)
        for h in range(group):
            at = (g * group + h) * HEAD_WIDTH
            out_ref[:, at : at + HEAD_WIDTH] = mine[h * rows : (h + 1) * rows]


def attend_kernel(sources, n_ctx, kv_dev, valid_ref, *refs):
    query_refs, refs = refs[:sources], refs[sources:]
    cache_refs, out_refs = refs[:n_ctx], refs[n_ctx:]
    shard_len = valid_ref.shape[1]
    span = kv_dev * HEAD_WIDTH
    pieces = shard_len // span

    def scale_row(scales, row):
        return jnp.concatenate(
            [scales[row * pieces + at : row * pieces + at + 1, :] for at in range(pieces)], axis=1
        )

    rows_doc = query_refs[0].shape[0] // kv_dev
    signs = sign_matrix()
    scale = 1.0 / math.sqrt(HEAD_WIDTH)
    groups = range(kv_dev)
    spans = [slice(g * rows_doc, (g + 1) * rows_doc) for g in groups]
    heads = [slice(g * HEAD_WIDTH, (g + 1) * HEAD_WIDTH) for g in groups]
    rows = [jnp.concatenate([ref[span, :] for ref in query_refs], axis=0) for span in spans]
    states = [None] * kv_dev
    for first in range(0, n_ctx, 2):
        steps = range(first, min(first + 2, n_ctx))
        scales = {step: cache_refs[step][2 * shard_len :, :].astype(jnp.float32) for step in steps}
        valid = {step: valid_ref[step : step + 1, :] > 0.0 for step in steps}
        scores = {}
        for g in groups:
            for step in steps:
                key_scale = scale_row(scales[step], g) * (scale * math.log2(math.e))
                product = lax.dot_general(
                    rows[g],
                    cache_refs[step][:shard_len, heads[g]],
                    (((1,), (1,)), ((), ())),
                    preferred_element_type=jnp.float32,
                )
                scores[g, step] = jnp.where(valid[step], product * key_scale, -1e30)
        tops = []
        for g in groups:
            top = functools.reduce(
                jnp.maximum, [jnp.max(scores[g, step], axis=-1, keepdims=True) for step in steps]
            )
            tops.append(top if states[g] is None else jnp.maximum(top, states[g][0]))
        for g in groups:
            all_probs, summed = 0.0, 0.0
            for step in steps:
                value_scale = scale_row(scales[step], kv_dev + g)
                probs = jnp.exp2(scores[g, step] - tops[g])
                all_probs = all_probs + probs
                weights = (probs * value_scale).astype(jnp.bfloat16)
                summed = summed + jnp.dot(
                    weights,
                    cache_refs[step][shard_len : 2 * shard_len, heads[g]],
                    preferred_element_type=jnp.float32,
                )
            total = jnp.sum(all_probs, axis=-1, keepdims=True)
            if states[g] is not None:
                factor = jnp.exp2(states[g][0] - tops[g])
                total = total + states[g][1] * factor
                summed = summed + states[g][2] * factor
            states[g] = (tops[g], total, summed)
    for g in groups:
        _, total, summed = states[g]
        mixed = summed * (scale / total)
        high = mixed.astype(jnp.bfloat16)
        low = (mixed - high.astype(jnp.float32)).astype(jnp.bfloat16)
        result = jnp.dot(high, signs, preferred_element_type=jnp.float32) + jnp.dot(
            low, signs, preferred_element_type=jnp.float32
        )
        result = result.astype(jnp.bfloat16)
        for k in range(sources):
            out_refs[k][spans[g], :] = result[k * rows_doc : (k + 1) * rows_doc]


def assemble_kernel(n_head, steps, *refs):
    block_refs, out_ref, sems = refs[: len(steps)], refs[-2], refs[-1]
    me = lax.axis_index("head")
    width = block_refs[0].shape[1]
    copies = []
    for at, step in enumerate(steps):
        column = pl.multiple_of(peer_of_traced(me, step, n_head) * width, width)
        copies.append(
            pltpu.make_async_copy(block_refs[at], out_ref.at[:, pl.ds(column, width)], sems.at[at])
        )
    for copy in copies:
        copy.start()
    for copy in copies:
        copy.wait()


def peer_of_traced(index, step, count):
    if count & (count - 1) == 0:
        return index ^ step
    return lax.rem(index + step, count)


def shards(
    queries,
    doc_of,
    doc_lengths,
    rotated_key_levels,
    rotated_value_levels,
    key_level_scale,
    value_level_scale,
):
    rows_home, width = queries.shape
    heads_dev = width // HEAD_WIDTH
    kv_dev = key_level_scale.shape[1]
    shard_len = rotated_key_levels.shape[1]
    n_doc = lax.axis_size("doc")
    n_ctx = lax.axis_size("ctx")
    n_head = lax.axis_size("head")
    cap = max(2, 3 * rows_home // (2 * n_doc))
    params = pltpu.CompilerParams(vmem_limit_bytes=VMEM_BYTES)
    vmem = pl.BlockSpec(memory_space=pltpu.VMEM)
    slots = heads_dev * cap
    slot_block = jax.ShapeDtypeStruct((slots, HEAD_WIDTH), jnp.bfloat16)

    key_block, value_block = rotated_key_levels[0], rotated_value_levels[0]
    args = (
        doc_of.reshape(1, rows_home),
        doc_lengths.reshape(1, doc_lengths.shape[0]),
        queries,
        key_block,
        value_block,
        key_level_scale[0],
        value_level_scale[0],
    )
    placing_block = jax.ShapeDtypeStruct((n_doc * (LANES // rows_home) * cap, LANES), jnp.bfloat16)
    hbm = pl.BlockSpec(memory_space=pltpu.HBM)
    anywhere = pl.BlockSpec(memory_space=pl.ANY)
    cache_rows = 2 * shard_len + 2 * shard_len // HEAD_WIDTH
    placing, valid, own_cache, *outgoing = pl.pallas_call(
        functools.partial(dispatch_kernel, n_doc, n_ctx, cap),
        out_shape=[
            placing_block,
            jax.ShapeDtypeStruct((n_ctx, shard_len), jnp.float32),
            jax.ShapeDtypeStruct((cache_rows, kv_dev * HEAD_WIDTH), key_block.dtype),
        ]
        + [slot_block] * n_doc,
        in_specs=[hbm] * len(args),
        out_specs=[vmem] * (n_doc + 3),
        scratch_shapes=[
            pltpu.VMEM(args[at].shape, args[at].dtype) for at in (0, 1, 2, 5, 6)
        ]
        + [pltpu.SemaphoreType.DMA((len(args),))],
        compiler_params=params,
    )(*[pltpu.with_memory_space_constraint(arg, pltpu.HBM) for arg in args])
    cache = [own_cache]
    for step in range(1, n_ctx):
        cache.append(
            lax.ppermute(own_cache, "ctx", [(i, (i + step) % n_ctx) for i in range(n_ctx)])
        )
    arrived = [outgoing[0]] + [sent(outgoing[k], "doc", k) for k in range(1, n_doc)]

    def attended_for(steps, valid):
        sources = [arrived[k] for k in steps]
        rows = len(sources) * slots
        return pl.pallas_call(
            functools.partial(attend_kernel, len(sources), n_ctx, kv_dev),
            out_shape=[slot_block] * len(sources),
            in_specs=[vmem] * (1 + len(sources) + n_ctx),
            out_specs=[vmem] * len(sources),
            compiler_params=params,
            cost_estimate=pl.CostEstimate(
                flops=4 * rows * n_ctx * shard_len * HEAD_WIDTH,
                bytes_accessed=4 * n_ctx * shard_len * kv_dev * HEAD_WIDTH,
                transcendentals=rows * n_ctx * shard_len,
            ),
        )(valid, *sources, *cache)

    finished = {}
    for step in sorted(range(1, n_doc), key=lambda step: (step % 2, step)):
        finished[step] = attended_for((step,), valid)[0]
        finished[step], valid = lax.optimization_barrier((finished[step], valid))
    finished[0] = attended_for((0,), valid)[0]
    back = [finished[0]] + [returned(finished[k], "doc", k) for k in range(1, n_doc)]

    turned = pl.pallas_call(
        turn_kernel,
        out_shape=jax.ShapeDtypeStruct(placing.shape[::-1], placing.dtype),
        in_specs=[vmem, anywhere],
        out_specs=vmem,
        compiler_params=params,
    )(placing, finished[0])
    mine = pl.pallas_call(
        functools.partial(collect_kernel, n_doc, cap),
        out_shape=jax.ShapeDtypeStruct((rows_home, width), jnp.bfloat16),
        in_specs=[vmem] * (1 + n_doc),
        out_specs=vmem,
        compiler_params=params,
    )(turned, *back)

    def assembled(steps, before):
        return pl.pallas_call(
            functools.partial(assemble_kernel, n_head, steps),
            out_shape=jax.ShapeDtypeStruct((rows_home, n_head * width), jnp.bfloat16),
            in_specs=[anywhere] * len(steps) + [hbm] * len(before),
            out_specs=hbm,
            scratch_shapes=[pltpu.SemaphoreType.DMA((len(steps),))],
            input_output_aliases={len(steps): 0} if before else {},
            compiler_params=params,
        )(*[blocks[step] for step in steps], *before)

    order = sorted(range(1, n_head), key=lambda step: (step % 2, step))
    blocks = {0: mine}
    for step in order:
        blocks[step] = returned(mine, "head", step)
    if len(order) < 2:
        return assembled([0] + order, ())
    attended = assembled([0, order[0]], ())
    for step in order[1:]:
        attended = assembled([step], (attended,))
    return attended


def solution(mesh):
    in_specs = (
        P(("doc", "ctx"), "head"),
        P(("doc", "ctx"), None),
        P(),
        P("doc", "ctx", "head"),
        P("doc", "ctx", "head"),
        P("doc", "head", "ctx"),
        P("doc", "head", "ctx"),
    )
    out_specs = P(("doc", "ctx"), None)
    return jax.shard_map(shards, mesh=mesh, in_specs=in_specs, out_specs=out_specs, check_vma=False)
```

```python
import functools
import math

import jax
import jax.numpy as jnp
from jax import lax
from jax.experimental import pallas as pl
from jax.experimental.pallas import tpu as pltpu
from jax.sharding import PartitionSpec as P

HEAD_WIDTH = 128
LANES = 128
VMEM_BYTES = 40 * 1024 * 1024


def peer_of(index, step, count):
    if count & (count - 1) == 0:
        return index ^ step
    return (index + step) % count


def sent(value, axis, step):
    count = lax.axis_size(axis)
    return lax.ppermute(value, axis, [(i, peer_of(i, step, count)) for i in range(count)])


def returned(value, axis, step):
    count = lax.axis_size(axis)
    return lax.ppermute(value, axis, [(peer_of(i, step, count), i) for i in range(count)])


def sign_matrix():
    row = lax.broadcasted_iota(jnp.int32, (HEAD_WIDTH, HEAD_WIDTH), 0)
    column = lax.broadcasted_iota(jnp.int32, (HEAD_WIDTH, HEAD_WIDTH), 1)
    both = row & column
    both = both ^ (both >> 4)
    both = both ^ (both >> 2)
    both = both ^ (both >> 1)
    return (1 - 2 * (both & 1)).astype(jnp.float32).astype(jnp.bfloat16)


def placing_matrix(doc_row, n_doc, cap):
    rows = doc_row.shape[1]
    group = LANES // rows
    me = lax.axis_index("doc")
    square = (rows, rows)
    diagonal = lax.broadcasted_iota(jnp.int32, square, 0) == lax.broadcasted_iota(
        jnp.int32, square, 1
    )
    doc_column = jnp.sum(
        jnp.where(diagonal, jnp.broadcast_to(doc_row, square), 0), axis=1, keepdims=True
    )
    request = lax.broadcasted_iota(jnp.int32, (rows, LANES), 0)
    lane = lax.broadcasted_iota(jnp.int32, (rows, LANES), 1)
    docs = jnp.broadcast_to(doc_column, (rows, LANES))
    lane_request = lane % rows
    lane_doc = jnp.sum(jnp.where(request == lane_request, docs, 0), axis=0, keepdims=True)
    rank = jnp.sum(
        jnp.where((docs == lane_doc) & (request < lane_request), 1, 0), axis=0, keepdims=True
    )
    if n_doc & (n_doc - 1) == 0:
        step = lane_doc ^ me
    else:
        step = (lane_doc - me + n_doc) % n_doc
    place = step * (group * cap) + (lane[:1] // rows) * cap + rank
    slots = n_doc * group * cap
    slot = lax.broadcasted_iota(jnp.int32, (slots, LANES), 0)
    return jnp.where(slot == place, 1.0, 0.0).astype(jnp.bfloat16)


def dispatch_kernel(
    n_doc,
    n_ctx,
    cap,
    doc_hbm,
    length_hbm,
    query_hbm,
    key_hbm,
    value_hbm,
    key_scale_hbm,
    value_scale_hbm,
    placing_ref,
    valid_ref,
    cache_ref,
    *refs,
):
    out_refs, (doc_ref, length_ref, query_ref, key_scale_ref, value_scale_ref, sems) = (
        refs[:n_doc],
        refs[n_doc:],
    )
    shard_len, span = key_hbm.shape
    pairs = (
        (query_hbm, query_ref),
        (doc_hbm, doc_ref),
        (key_hbm, cache_ref.at[pl.ds(0, shard_len)]),
        (value_hbm, cache_ref.at[pl.ds(shard_len, shard_len)]),
        (key_scale_hbm, key_scale_ref),
        (value_scale_hbm, value_scale_ref),
        (length_hbm, length_ref),
    )
    copies = [
        pltpu.make_async_copy(source, target, sems.at[at])
        for at, (source, target) in enumerate(pairs)
    ]
    for copy in copies:
        copy.start()
    rows, width = query_ref.shape
    group = LANES // rows
    heads = width // HEAD_WIDTH
    block = group * cap
    signs = sign_matrix()
    scale = 1.0 / math.sqrt(HEAD_WIDTH)
    copies[1].wait()
    placing = placing_matrix(doc_ref[...], n_doc, cap)
    placing_ref[...] = placing
    copies[0].wait()
    rotated = []
    for g in range(heads // group):
        stacked = jnp.concatenate(
            [
                query_ref[:, (g * group + h) * HEAD_WIDTH : (g * group + h + 1) * HEAD_WIDTH]
                for h in range(group)
            ],
            axis=0,
        )
        product = jnp.dot(stacked, signs, preferred_element_type=jnp.float32) * scale
        rotated.append(product.astype(jnp.bfloat16))
    for g in range(heads // group):
        placed = jnp.dot(placing, rotated[g], preferred_element_type=jnp.float32).astype(
            jnp.bfloat16
        )
        for k in range(n_doc):
            out_refs[k][g * block : (g + 1) * block, :] = placed[k * block : (k + 1) * block]
    for copy in copies[4:]:
        copy.wait()
    scale_rows = []
    for scale_ref in (key_scale_ref, value_scale_ref):
        scales = scale_ref[...].astype(jnp.float32)
        scale_rows += [
            scales[row : row + 1, at : at + span]
            for row in range(scales.shape[0])
            for at in range(0, shard_len, span)
        ]
    cache_ref[2 * shard_len :, :] = jnp.concatenate(scale_rows, axis=0).astype(jnp.bfloat16)
    lengths = length_ref[...]
    lane = lax.broadcasted_iota(jnp.int32, lengths.shape, 1)
    length = jnp.sum(
        jnp.where(lane == lax.axis_index("doc"), lengths, 0), axis=1, keepdims=True
    )
    step = lax.broadcasted_iota(jnp.int32, valid_ref.shape, 0)
    anchor = (lax.axis_index("ctx") - step + n_ctx) % n_ctx
    position = lax.broadcasted_iota(jnp.int32, valid_ref.shape, 1) + anchor * shard_len
    valid_ref[...] = jnp.where(position < length, 1.0, 0.0)
    for copy in copies[2:4]:
        copy.wait()


def turn_kernel(placing_ref, after_ref, out_ref):
    out_ref[...] = placing_ref[...].astype(jnp.float32).T.astype(jnp.bfloat16)


def collect_kernel(n_doc, cap, placing_ref, *refs):
    back_refs, out_ref = refs[:n_doc], refs[n_doc]
    rows, width = out_ref.shape
    group = LANES // rows
    heads = width // HEAD_WIDTH
    block = group * cap
    placing = placing_ref[...]
    for g in range(heads // group):
        slots = jnp.concatenate(
            [back_refs[k][g * block : (g + 1) * block, :] for k in range(n_doc)], axis=0
        )
        mine = jnp.dot(placing, slots, preferred_element_type=jnp.float32).astype(jnp.bfloat16)
        for h in range(group):
            at = (g * group + h) * HEAD_WIDTH
            out_ref[:, at : at + HEAD_WIDTH] = mine[h * rows : (h + 1) * rows]


def attend_kernel(sources, n_ctx, kv_dev, valid_ref, *refs):
    query_refs, refs = refs[:sources], refs[sources:]
    cache_refs, out_refs = refs[:n_ctx], refs[n_ctx:]
    shard_len = valid_ref.shape[1]
    span = kv_dev * HEAD_WIDTH
    pieces = shard_len // span

    def scale_row(scales, row):
        return jnp.concatenate(
            [scales[row * pieces + at : row * pieces + at + 1, :] for at in range(pieces)], axis=1
        )

    rows_doc = query_refs[0].shape[0] // kv_dev
    signs = sign_matrix()
    scale = 1.0 / math.sqrt(HEAD_WIDTH)
    groups = range(kv_dev)
    spans = [slice(g * rows_doc, (g + 1) * rows_doc) for g in groups]
    heads = [slice(g * HEAD_WIDTH, (g + 1) * HEAD_WIDTH) for g in groups]
    rows = [jnp.concatenate([ref[span, :] for ref in query_refs], axis=0) for span in spans]
    states = [None] * kv_dev
    for first in range(0, n_ctx, 2):
        steps = range(first, min(first + 2, n_ctx))
        scales = {step: cache_refs[step][2 * shard_len :, :].astype(jnp.float32) for step in steps}
        valid = {step: valid_ref[step : step + 1, :] > 0.0 for step in steps}
        scores = {}
        for g in groups:
            for step in steps:
                key_scale = scale_row(scales[step], g) * (scale * math.log2(math.e))
                product = lax.dot_general(
                    rows[g],
                    cache_refs[step][:shard_len, heads[g]],
                    (((1,), (1,)), ((), ())),
                    preferred_element_type=jnp.float32,
                )
                scores[g, step] = jnp.where(valid[step], product * key_scale, -1e30)
        tops = []
        for g in groups:
            top = functools.reduce(
                jnp.maximum, [jnp.max(scores[g, step], axis=-1, keepdims=True) for step in steps]
            )
            tops.append(top if states[g] is None else jnp.maximum(top, states[g][0]))
        for g in groups:
            all_probs, summed = 0.0, 0.0
            for step in steps:
                value_scale = scale_row(scales[step], kv_dev + g)
                probs = jnp.exp2(scores[g, step] - tops[g])
                all_probs = all_probs + probs
                weights = (probs * value_scale).astype(jnp.bfloat16)
                summed = summed + jnp.dot(
                    weights,
                    cache_refs[step][shard_len : 2 * shard_len, heads[g]],
                    preferred_element_type=jnp.float32,
                )
            total = jnp.sum(all_probs, axis=-1, keepdims=True)
            if states[g] is not None:
                factor = jnp.exp2(states[g][0] - tops[g])
                total = total + states[g][1] * factor
                summed = summed + states[g][2] * factor
            states[g] = (tops[g], total, summed)
    for g in groups:
        _, total, summed = states[g]
        mixed = summed * (scale / total)
        high = mixed.astype(jnp.bfloat16)
        low = (mixed - high.astype(jnp.float32)).astype(jnp.bfloat16)
        result = jnp.dot(high, signs, preferred_element_type=jnp.float32) + jnp.dot(
            low, signs, preferred_element_type=jnp.float32
        )
        result = result.astype(jnp.bfloat16)
        for k in range(sources):
            out_refs[k][spans[g], :] = result[k * rows_doc : (k + 1) * rows_doc]


def assemble_kernel(n_head, steps, *refs):
    block_refs, out_ref, sems = refs[: len(steps)], refs[-2], refs[-1]
    me = lax.axis_index("head")
    width = block_refs[0].shape[1]
    copies = []
    for at, step in enumerate(steps):
        column = pl.multiple_of(peer_of_traced(me, step, n_head) * width, width)
        copies.append(
            pltpu.make_async_copy(block_refs[at], out_ref.at[:, pl.ds(column, width)], sems.at[at])
        )
    for copy in copies:
        copy.start()
    for copy in copies:
        copy.wait()


def peer_of_traced(index, step, count):
    if count & (count - 1) == 0:
        return index ^ step
    return lax.rem(index + step, count)


def shards(
    queries,
    doc_of,
    doc_lengths,
    rotated_key_levels,
    rotated_value_levels,
    key_level_scale,
    value_level_scale,
):
    rows_home, width = queries.shape
    heads_dev = width // HEAD_WIDTH
    kv_dev = key_level_scale.shape[1]
    shard_len = rotated_key_levels.shape[1]
    n_doc = lax.axis_size("doc")
    n_ctx = lax.axis_size("ctx")
    n_head = lax.axis_size("head")
    cap = max(2, 3 * rows_home // (2 * n_doc))
    params = pltpu.CompilerParams(vmem_limit_bytes=VMEM_BYTES)
    vmem = pl.BlockSpec(memory_space=pltpu.VMEM)
    slots = heads_dev * cap
    slot_block = jax.ShapeDtypeStruct((slots, HEAD_WIDTH), jnp.bfloat16)

    key_block, value_block = rotated_key_levels[0], rotated_value_levels[0]
    args = (
        doc_of.reshape(1, rows_home),
        doc_lengths.reshape(1, doc_lengths.shape[0]),
        queries,
        key_block,
        value_block,
        key_level_scale[0],
        value_level_scale[0],
    )
    placing_block = jax.ShapeDtypeStruct((n_doc * (LANES // rows_home) * cap, LANES), jnp.bfloat16)
    hbm = pl.BlockSpec(memory_space=pltpu.HBM)
    anywhere = pl.BlockSpec(memory_space=pl.ANY)
    cache_rows = 2 * shard_len + 2 * shard_len // HEAD_WIDTH
    placing, valid, own_cache, *outgoing = pl.pallas_call(
        functools.partial(dispatch_kernel, n_doc, n_ctx, cap),
        out_shape=[
            placing_block,
            jax.ShapeDtypeStruct((n_ctx, shard_len), jnp.float32),
            jax.ShapeDtypeStruct((cache_rows, kv_dev * HEAD_WIDTH), key_block.dtype),
        ]
        + [slot_block] * n_doc,
        in_specs=[hbm] * len(args),
        out_specs=[vmem] * (n_doc + 3),
        scratch_shapes=[
            pltpu.VMEM(args[at].shape, args[at].dtype) for at in (0, 1, 2, 5, 6)
        ]
        + [pltpu.SemaphoreType.DMA((len(args),))],
        compiler_params=params,
    )(*[pltpu.with_memory_space_constraint(arg, pltpu.HBM) for arg in args])
    cache = [own_cache]
    for step in range(1, n_ctx):
        cache.append(
            lax.ppermute(own_cache, "ctx", [(i, (i + step) % n_ctx) for i in range(n_ctx)])
        )
    arrived = [outgoing[0]] + [sent(outgoing[k], "doc", k) for k in range(1, n_doc)]

    def attended_for(steps, valid):
        sources = [arrived[k] for k in steps]
        rows = len(sources) * slots
        return pl.pallas_call(
            functools.partial(attend_kernel, len(sources), n_ctx, kv_dev),
            out_shape=[slot_block] * len(sources),
            in_specs=[vmem] * (1 + len(sources) + n_ctx),
            out_specs=[vmem] * len(sources),
            compiler_params=params,
            cost_estimate=pl.CostEstimate(
                flops=4 * rows * n_ctx * shard_len * HEAD_WIDTH,
                bytes_accessed=4 * n_ctx * shard_len * kv_dev * HEAD_WIDTH,
                transcendentals=rows * n_ctx * shard_len,
            ),
        )(valid, *sources, *cache)

    finished = {}
    for step in sorted(range(1, n_doc), key=lambda step: (step % 2, step)):
        finished[step] = attended_for((step,), valid)[0]
        finished[step], valid = lax.optimization_barrier((finished[step], valid))
    finished[0] = attended_for((0,), valid)[0]
    back = [finished[0]] + [returned(finished[k], "doc", k) for k in range(1, n_doc)]

    turned = pl.pallas_call(
        turn_kernel,
        out_shape=jax.ShapeDtypeStruct(placing.shape[::-1], placing.dtype),
        in_specs=[vmem, anywhere],
        out_specs=vmem,
        compiler_params=params,
    )(placing, finished[0])
    mine = pl.pallas_call(
        functools.partial(collect_kernel, n_doc, cap),
        out_shape=jax.ShapeDtypeStruct((rows_home, width), jnp.bfloat16),
        in_specs=[vmem] * (1 + n_doc),
        out_specs=vmem,
        compiler_params=params,
    )(turned, *back)

    def assembled(steps, before):
        return pl.pallas_call(
            functools.partial(assemble_kernel, n_head, steps),
            out_shape=jax.ShapeDtypeStruct((rows_home, n_head * width), jnp.bfloat16),
            in_specs=[anywhere] * len(steps) + [hbm] * len(before),
            out_specs=hbm,
            scratch_shapes=[pltpu.SemaphoreType.DMA((len(steps),))],
            input_output_aliases={len(steps): 0} if before else {},
            compiler_params=params,
        )(*[blocks[step] for step in steps], *before)

    order = sorted(range(1, n_head), key=lambda step: (step % 2, step))
    blocks = {0: mine}
    for step in order:
        blocks[step] = returned(mine, "head", step)
    if len(order) < 2:
        return assembled([0] + order, ())
    attended = assembled([0, order[0]], ())
    for step in order[1:]:
        attended = assembled([step], (attended,))
    return attended


def solution(mesh):
    in_specs = (
        P(("doc", "ctx"), "head"),
        P(("doc", "ctx"), None),
        P(),
        P("doc", "ctx", "head"),
        P("doc", "ctx", "head"),
        P("doc", "head", "ctx"),
        P("doc", "head", "ctx"),
    )
    out_specs = P(("doc", "ctx"), None)
    return jax.shard_map(shards, mesh=mesh, in_specs=in_specs, out_specs=out_specs, check_vma=False)
```
